512 devices in a mesh: dp: 32 (over z, core), tensor: 16 (over y, x).
Axes of the slice: x: 4, y: 4, z: 16, core: 2. Of those that a mesh axis runs over, the one named last changes fastest.
Arguments:
- queries: bfloat16 [2048, 4, 32, 128], P(('dp', 'tensor')), may hold values from -160 to 160, as said below
- cached_key_rows: bfloat16 [2048, 4, 512, 128], P(('dp', 'tensor')), may hold values from -6 to 6
- cached_value_rows: bfloat16 [2048, 4, 512, 128], P(('dp', 'tensor')), may hold values from -24 to 24
- cache_fill_length: int32 [2048], P(('dp', 'tensor')), may hold values from 4 to 512, as said below
- request_adapters: int32 [2048], P('dp'), may hold values from 0 to 1023, as said below
- wo: bfloat16 [4096, 4096], P('tensor'), may hold values from -0.125 to 0.125
- adapter_down_weight: bfloat16 [1024, 16, 4096], P('dp', None, 'tensor'), may hold values from -0.09375 to 0.09375
- adapter_up_weight: bfloat16 [1024, 16, 4096], P('dp', None, 'tensor'), may hold values from -1.5 to 1.5
Outputs:
- layer_out: bfloat16 [2048, 4, 4096], P('dp', None, 'tensor')
The draws below stay inside these ranges and needn't reach their ends.
Inputs may be any that keep to these rules, and one draw needn't show every extreme that they name: `queries`: queries of order one; some may be far larger. `cache_fill_length`: 512 is reached by some request in every draw. `request_adapters`: adapter a is kept by dp index a // 32. Among the 64 requests of one dp index (aligned blocks of 64), at most 2 use adapters of one owner, and some owner gets exactly 2 in every block. Some adapters are far more popular than others.
All inputs are finite; a program needn't handle non-finite values.
Results may differ from the reference program's by a relative error of at most 0.006.
Values may be sent and summed in bfloat16 or wider, within the bound.
No kernel may reach another device: no remote copies, remote signals or barrier semaphores. Data moves between devices by JAX's collectives and lax.ppermute only.
A program may use at most 64 MiB of HBM per device.

```python
import math
import jax
import jax.numpy as jnp
from jax import lax

QUERY_HEADS = 32
KV_HEADS = 4
HEAD_SIZE = 128
OUTPUT_FEATURES = 4096
ADAPTER_RANK = 16
STEPS = 4
ADAPT_DEV = 32
CACHE = 512
GROUP = 64
REQS = 2048
CAP = 2
ADAPTER_COUNT = 1024


def shared_keys(key):
    drawn = jax.random.normal(jax.random.fold_in(key, 5), (REQS, KV_HEADS, CACHE, HEAD_SIZE), jnp.float32)
    return jnp.clip(drawn, -6.0, 6.0)


def draw_cached_key_rows(key, part):
    base_keys = shared_keys(key)
    return base_keys.astype(jnp.bfloat16)


def draw_queries(key, part):
    key = jax.random.fold_in(key, 22)
    fresh = jnp.clip(jax.random.normal(key, (REQS, STEPS, QUERY_HEADS, HEAD_SIZE), jnp.float32), -6.0, 6.0)
    return fresh.astype(jnp.bfloat16)


def draw_cache_fill_length(key, part):
    key = jax.random.fold_in(key, 31)
    key_len, key_top = jax.random.split(key)
    drawn = jax.random.randint(key_len, (REQS,), STEPS, CACHE + 1, jnp.int32)
    longest = jax.random.randint(key_top, (), 0, REQS, jnp.int32)
    return jnp.where(jnp.arange(REQS, dtype=jnp.int32) == longest, CACHE, drawn).astype(jnp.int32)


def draw_request_adapters(key, part):
    key = jax.random.fold_in(key, 41)
    key_owner, key_local = jax.random.split(key)
    block_count = REQS // GROUP
    orders = jax.vmap(lambda single: jax.random.permutation(single, block_count))(jax.random.split(key_owner, block_count)).astype(jnp.int32)
    position = jnp.arange(GROUP, dtype=jnp.int32) // CAP
    owner_ids = orders[:, position]
    factors = jax.random.randint(key_local, (block_count, GROUP, 3), 0, ADAPT_DEV, jnp.int32)
    local_ids = factors[:, :, 0] * factors[:, :, 1] * factors[:, :, 2] // (ADAPT_DEV * ADAPT_DEV)
    return (owner_ids * ADAPT_DEV + local_ids).reshape(REQS).astype(jnp.int32)


def with_spikes(array, rng, source, target, blocks, factor):
    owner, partner = [(jnp.arange(array.shape[dim]) // (array.shape[dim] // blocks)).reshape([-1 if axis == dim else 1 for axis in range(array.ndim)]) for dim in (source, target)]
    chosen = jax.random.permutation(rng, blocks)[partner]
    strong = (owner == chosen) | (owner == (partner + blocks // 2) % blocks)
    return jnp.where(strong, factor * array, array)


def level_of(rng, extent, cuts, smallest, largest):
    def one(dim, shards_of):
        heights = jax.random.uniform(jax.random.fold_in(jax.random.fold_in(rng, 6), dim), (shards_of,), jnp.float32, smallest / len(cuts), largest / len(cuts))
        return jnp.repeat(jnp.exp(heights), extent[dim] // shards_of).reshape((-1,) + (1,) * (len(extent) - dim - 1))

    level = one(*cuts[0])
    for cut in cuts[1:]:
        level = level * one(*cut)
    return level


def gaussian(rng, dims, spread, limit, cuts=(), held_as=jnp.bfloat16):
    array = jax.random.normal(rng, dims, jnp.float32) * spread
    if len(cuts) > 0:
        array = level_of(rng, dims, cuts, -0.22, 0.18) * array
    return jnp.clip(array, min=-limit, max=limit).astype(held_as)


def heavy_noise(rng, dims, scale, bound, shards, heavy, kind=jnp.bfloat16):
    result = scale * jax.random.normal(rng, dims, jnp.float32)
    if shards:
        result = result * level_of(rng, dims, shards, -0.22, 0.18)
    return jnp.clip(with_spikes(result, jax.random.fold_in(rng, 3), *heavy), -bound, bound).astype(kind)


def setup_inputs(seed: int = 0) -> dict:
    keys = jax.random.split(jax.random.key(seed), 9)
    return {
        "queries": draw_queries(jax.random.fold_in(keys[8], 71), 0),
        "cached_key_rows": draw_cached_key_rows(jax.random.fold_in(keys[8], 71), 0),
        "cached_value_rows": gaussian(keys[2], (REQS, KV_HEADS, CACHE, HEAD_SIZE), 4.0, 24.0, ((0, 512),)),
        "cache_fill_length": draw_cache_fill_length(jax.random.fold_in(keys[8], 71), 0),
        "request_adapters": draw_request_adapters(jax.random.fold_in(keys[8], 71), 0),
        "wo": heavy_noise(keys[5], (QUERY_HEADS * HEAD_SIZE, OUTPUT_FEATURES), (QUERY_HEADS * HEAD_SIZE) ** -0.5, 0.125, ((0, 16),), (0, 1, 16, 2.0)),
        "adapter_down_weight": gaussian(keys[6], (ADAPTER_COUNT, ADAPTER_RANK, QUERY_HEADS * HEAD_SIZE), (QUERY_HEADS * HEAD_SIZE) ** -0.5, 0.09375, ((0, 32), (2, 16))),
        "adapter_up_weight": gaussian(keys[7], (ADAPTER_COUNT, ADAPTER_RANK, OUTPUT_FEATURES), ADAPTER_RANK ** -0.5, 1.5, ((0, 32), (2, 16))),
    }


NEG_FILL = -1e+30

def attend(queries, cached_key_rows, cached_value_rows, cache_fill_length):
    requests, steps, heads, head_dim = queries.shape
    kv_heads = cached_key_rows.shape[1]
    cache_len = cached_key_rows.shape[2]
    per_group = heads // kv_heads
    grouped = queries.reshape(requests, steps, kv_heads, per_group, head_dim).astype(jnp.float32)
    scores = jnp.einsum('rskgd,rkpd->rskgp', grouped, cached_key_rows.astype(jnp.float32)) / math.sqrt(head_dim)
    positions = jnp.arange(cache_len, dtype=jnp.int32)
    last_pos = cache_fill_length[:, None] - steps + jnp.arange(steps, dtype=jnp.int32)[None, :]
    valid_mask = positions[None, None, :] <= last_pos[:, :, None]
    scores = jnp.where(valid_mask[:, :, None, None, :], scores, NEG_FILL)
    highest = lax.optimization_barrier(jnp.max(scores, axis=-1, keepdims=True))
    raised = jnp.exp(scores - highest)
    weights = (raised / lax.optimization_barrier(jnp.sum(raised, axis=-1, keepdims=True))).astype(jnp.bfloat16)
    attended = jnp.einsum('rskgp,rkpd->rskgd', weights.astype(jnp.float32), cached_value_rows.astype(jnp.float32))
    return attended.astype(jnp.bfloat16).reshape(requests, steps, heads, head_dim)

def reference(queries, cached_key_rows, cached_value_rows, cache_fill_length, request_adapters, wo, adapter_down_weight, adapter_up_weight):
    blocks = REQS // GROUP

    def per_block(pieces):
        return attend(pieces[0], pieces[1], pieces[2], pieces[3])
    attended = lax.map(per_block, (queries.reshape((blocks, GROUP) + queries.shape[1:]), cached_key_rows.reshape((blocks, GROUP) + cached_key_rows.shape[1:]), cached_value_rows.reshape((blocks, GROUP) + cached_value_rows.shape[1:]), cache_fill_length.reshape(blocks, GROUP)))
    head_cols = attended.reshape(REQS, STEPS, QUERY_HEADS * HEAD_SIZE)
    base_output = jnp.dot(head_cols.reshape(REQS * STEPS, QUERY_HEADS * HEAD_SIZE), wo, preferred_element_type=jnp.float32).reshape(REQS, STEPS, OUTPUT_FEATURES)
    down_weight_rows = adapter_down_weight[request_adapters].astype(jnp.float32)
    rank_projection = jnp.einsum('qsc,qrc->qsr', head_cols.astype(jnp.float32), down_weight_rows).astype(jnp.bfloat16)
    up_weight_rows = adapter_up_weight[request_adapters].astype(jnp.float32)
    adapter_delta = jnp.einsum('kom,kmx->kox', rank_projection.astype(jnp.float32), up_weight_rows)
    return (base_output + adapter_delta).astype(jnp.bfloat16)
```

```python
import functools
import math

import jax
import jax.numpy as jnp
from jax import lax
from jax.experimental import pallas as pl
from jax.experimental.pallas import tpu as pltpu
from jax.sharding import PartitionSpec as P

NEG_FILL = -1e30
SIDE = 4


def attend(queries, cached_key_rows, cached_value_rows, cache_fill_length):
    requests, steps, heads, head_dim = queries.shape
    kv_heads = cached_key_rows.shape[1]
    cache_len = cached_key_rows.shape[2]
    per_group = heads // kv_heads
    grouped = queries.reshape(requests, steps, kv_heads, per_group, head_dim)
    scores = jnp.einsum(
        "rskgd,rkpd->rskgp", grouped, cached_key_rows, preferred_element_type=jnp.float32
    ) / math.sqrt(head_dim)
    positions = jnp.arange(cache_len, dtype=jnp.int32)
    last_pos = cache_fill_length[:, None] - steps + jnp.arange(steps, dtype=jnp.int32)[None, :]
    valid_mask = positions[None, None, :] <= last_pos[:, :, None]
    scores = jnp.where(valid_mask[:, :, None, None, :], scores, NEG_FILL)
    highest = jnp.max(scores, axis=-1, keepdims=True)
    raised = jnp.exp(scores - highest)
    weights = (raised / jnp.sum(raised, axis=-1, keepdims=True)).astype(jnp.bfloat16)
    attended = jnp.einsum(
        "rskgp,rkpd->rskgd", weights, cached_value_rows, preferred_element_type=jnp.float32
    )
    return attended.astype(jnp.bfloat16).reshape(requests, steps, heads, head_dim)


def project_kernel(place_ref, rows_ref, *refs):
    wo_refs, out_refs = refs[:SIDE], refs[SIDE:]
    step = pl.program_id(0)
    for s in range(SIDE):

        @pl.when(step == s)
        def _(s=s):
            for u in range(SIDE):
                part = jnp.dot(
                    rows_ref[...], wo_refs[u][...], preferred_element_type=jnp.float32
                )
                out_refs[s][u] = part.astype(out_refs[s].dtype)


def project(head_rows, wo, place):
    rows, depth = head_rows.shape
    width = wo.shape[1] // (SIDE * SIDE)

    def wo_block(u):
        def index_map(s, place_ref):
            x = lax.rem(place_ref[1] + s, SIDE)
            y = lax.rem(place_ref[0] + u, SIDE)
            return (0, y * SIDE + x)

        return pl.BlockSpec((depth, width), index_map)

    def whole(*shape):
        return pl.BlockSpec(shape, lambda s, place_ref: (0,) * len(shape))

    kinds = [jnp.float32] + [jnp.bfloat16] * (SIDE - 1)
    return pl.pallas_call(
        project_kernel,
        grid_spec=pltpu.PrefetchScalarGridSpec(
            num_scalar_prefetch=1,
            grid=(SIDE,),
            in_specs=[whole(rows, depth)] + [wo_block(u) for u in range(SIDE)],
            out_specs=[whole(SIDE, rows, width) for _ in kinds],
        ),
        out_shape=[jax.ShapeDtypeStruct((SIDE, rows, width), kind) for kind in kinds],
        compiler_params=pltpu.CompilerParams(vmem_limit_bytes=32 * 1024 * 1024),
        cost_estimate=pl.CostEstimate(
            flops=2 * rows * depth * wo.shape[1],
            bytes_accessed=2 * wo.size + 2 * rows * wo.shape[1],
            transcendentals=0,
        ),
        name="project",
    )(place, head_rows, *([wo] * SIDE))


def shift_x(value, s):
    pairs = [
        (y * SIDE + x, y * SIDE + (x + s) % SIDE) for y in range(SIDE) for x in range(SIDE)
    ]
    return lax.ppermute(value, "tensor", pairs)


def shift_y(value, s):
    pairs = [
        (y * SIDE + x, ((y + s) % SIDE) * SIDE + x) for y in range(SIDE) for x in range(SIDE)
    ]
    return lax.ppermute(value, "tensor", pairs)


def summed_projection(head_rows, wo, place):
    own, *others = project(head_rows, wo, place)
    arrived = [shift_x(part, s + 1) for s, part in enumerate(others)]
    along_x = [
        own[u] + sum(part[u].astype(jnp.float32) for part in arrived) for u in range(SIDE)
    ]
    arrived = [shift_y(along_x[u].astype(jnp.bfloat16), u) for u in range(1, SIDE)]
    return along_x[0] + sum(part.astype(jnp.float32) for part in arrived)


def on_device(
    queries,
    cached_key_rows,
    cached_value_rows,
    cache_fill_length,
    request_adapters,
    wo,
    adapter_down_weight,
    adapter_up_weight,
):
    owners = lax.axis_size("dp")
    shares = lax.axis_size("tensor")
    group_size = request_adapters.shape[0]
    owner_partial, rank, width = adapter_down_weight.shape
    capacity = group_size // owners
    steps = queries.shape[1]
    rows = group_size * steps
    tensor_index = lax.axis_index("tensor").astype(jnp.int32)
    place = jnp.stack([tensor_index // SIDE, tensor_index % SIDE])

    owner_ids = request_adapters // owner_partial
    local_ids = request_adapters % owner_partial
    order = jnp.arange(group_size, dtype=jnp.int32)
    earlier = (owner_ids[:, None] == owner_ids[None, :]) & (order[:, None] > order[None, :])
    slots = owner_ids * capacity + jnp.sum(earlier.astype(jnp.int32), axis=1)
    row_slots = (slots[:, None] * steps + jnp.arange(steps, dtype=jnp.int32)).reshape(rows)
    to_slots = (jnp.arange(rows, dtype=jnp.int32)[:, None] == row_slots[None, :]).astype(
        jnp.bfloat16
    )
    row_locals = jnp.repeat(local_ids, steps).astype(jnp.bfloat16)
    id_lanes = jnp.broadcast_to(row_locals[:, None], (rows, 128))

    attended = attend(queries, cached_key_rows, cached_value_rows, cache_fill_length)
    by_heads = lax.all_to_all(attended, "tensor", split_axis=2, concat_axis=0, tiled=True)
    head_rows = by_heads.reshape(rows, width)

    payload = jnp.dot(
        to_slots,
        jnp.concatenate([head_rows, id_lanes], axis=1),
        preferred_element_type=jnp.float32,
    ).astype(jnp.bfloat16)
    owned = lax.all_to_all(
        payload.reshape(owners, capacity * steps, width + 128), "dp", 0, 0, tiled=True
    ).reshape(rows, width + 128)
    owned_rows = owned[:, :width]
    owned_ids = owned[:, width : width + 1].astype(jnp.int32)
    columns = jnp.arange(owner_partial * rank, dtype=jnp.int32)
    chosen = owned_ids == (columns // rank)[None, :]
    fold = (jnp.arange(rank, dtype=jnp.int32)[:, None] == (columns % rank)[None, :]).astype(
        jnp.float32
    )
    every_down = jnp.einsum(
        "qc,kc->qk",
        owned_rows,
        adapter_down_weight.reshape(owner_partial * rank, width),
        preferred_element_type=jnp.float32,
    )
    partial_shrink = jnp.einsum(
        "mk,qk->mq",
        fold,
        jnp.where(chosen, every_down, 0.0),
        precision=lax.Precision.HIGHEST,
        preferred_element_type=jnp.float32,
    )
    partials = lax.all_to_all(
        jnp.broadcast_to(partial_shrink[None], (shares, rank, rows)), "tensor", 0, 0, tiled=True
    )
    shrink = jnp.sum(partials, axis=0).astype(jnp.bfloat16)
    spread = jnp.einsum(
        "mq,mk->qk", shrink, fold.astype(jnp.bfloat16), preferred_element_type=jnp.float32
    )
    delta = jnp.dot(
        jnp.where(chosen, spread, 0.0).astype(jnp.bfloat16),
        adapter_up_weight.reshape(owner_partial * rank, width),
        preferred_element_type=jnp.float32,
    ).astype(jnp.bfloat16)
    returned = lax.all_to_all(
        delta.reshape(owners, capacity * steps, width), "dp", 0, 0, tiled=True
    ).reshape(rows, width)

    base_output = summed_projection(head_rows, wo, place)
    adapter_delta = jnp.einsum(
        "sq,sd->qd", to_slots, returned, preferred_element_type=jnp.float32
    )
    return (base_output + adapter_delta).astype(jnp.bfloat16).reshape(group_size, steps, width)


def solution(mesh):
    in_specs = (
        P(("dp", "tensor"), None, None, None),
        P(("dp", "tensor"), None, None, None),
        P(("dp", "tensor"), None, None, None),
        P(("dp", "tensor")),
        P("dp"),
        P("tensor", None),
        P("dp", None, "tensor"),
        P("dp", None, "tensor"),
    )
    out_specs = P("dp", None, "tensor")
    return jax.shard_map(
        on_device, mesh=mesh, in_specs=in_specs, out_specs=out_specs, check_vma=False
    )
```

```python
import math

import jax
import jax.numpy as jnp
from jax import lax
from jax.experimental import pallas as pl
from jax.experimental.pallas import tpu as pltpu
from jax.sharding import PartitionSpec as P

NEG_FILL = -1e30
SIDE = 4


def attend_kernel(
    fill_ref, queries_ref, keys_ref, values_ref, out_ref,
    query_buf, key_buf, value_buf, score_buf, weight_buf, grouped_buf, query_sem, key_sem, value_sem,
):
    requests, steps, heads, head_dim = query_buf.shape
    kv_heads, cache_len = key_buf.shape[1], key_buf.shape[2]
    per_group = heads // kv_heads
    group_rows = steps * per_group
    width = 2 * head_dim
    query_copy = pltpu.make_async_copy(queries_ref, query_buf, query_sem)
    key_copies = [
        pltpu.make_async_copy(keys_ref.at[r], key_buf.at[r], key_sem.at[r]) for r in range(requests)
    ]
    value_copies = [
        pltpu.make_async_copy(values_ref.at[r], value_buf.at[r], value_sem.at[r])
        for r in range(requests)
    ]
    query_copy.start()
    for copy in key_copies + value_copies:
        copy.start()
    position = lax.broadcasted_iota(jnp.int32, (group_rows, cache_len), 1)
    step_of = lax.broadcasted_iota(jnp.int32, (group_rows, cache_len), 0) // per_group
    reach = position + steps - step_of
    query_copy.wait()
    for r in range(requests):
        every = query_buf[r].astype(jnp.float32)
        key_copies[r].wait()
        for k in range(kv_heads):
            grouped = every[:, k * per_group : (k + 1) * per_group, :]
            grouped = grouped.reshape(group_rows, head_dim).astype(jnp.bfloat16)
            score_buf[r * kv_heads + k] = lax.dot_general(
                grouped,
                key_buf[r, k],
                (((1,), (1,)), ((), ())),
                preferred_element_type=jnp.float32,
            )
    for r in range(requests):
        valid = reach <= fill_ref[r]
        for k in range(kv_heads):
            scores = score_buf[r * kv_heads + k] * (1.0 / math.sqrt(head_dim))
            scores = jnp.where(valid, scores, NEG_FILL)
            raised = jnp.exp(scores - jnp.max(scores, axis=1, keepdims=True))
            weights = raised * (1.0 / jnp.sum(raised, axis=1, keepdims=True))
            weight_buf[r * kv_heads + k] = weights.astype(jnp.bfloat16)
    for r in range(requests):
        value_copies[r].wait()
        for k in range(kv_heads):
            grouped_buf[r * kv_heads + k] = jnp.dot(
                weight_buf[r * kv_heads + k], value_buf[r, k], preferred_element_type=jnp.float32
            )
    for block in range(heads // 2):
        k, first = block * 2 // per_group, block * 2 % per_group
        halves = []
        for j in range(2):
            pieces = [
                grouped_buf[r * kv_heads + k, pl.ds(first + j, steps, stride=per_group), :]
                for r in range(requests)
            ]
            halves.append(jnp.concatenate(pieces, axis=0))
        part = jnp.concatenate(halves, axis=1).astype(jnp.bfloat16)
        out_ref[block, :, :width] = part
        out_ref[block ^ SIDE, :, width:] = part


def attend(queries, cached_key_rows, cached_value_rows, cache_fill_length):
    requests, steps, heads, head_dim = queries.shape
    kv_heads, cache_len = cached_key_rows.shape[1:3]
    blocks, rows = heads // 2, requests * steps
    pairs, group_rows = requests * kv_heads, steps * heads // kv_heads
    distant = pl.BlockSpec(memory_space=pltpu.HBM)
    return pl.pallas_call(
        attend_kernel,
        in_specs=[pl.BlockSpec(memory_space=pltpu.SMEM), distant, distant, distant],
        out_specs=pl.BlockSpec(memory_space=pltpu.VMEM),
        out_shape=jax.ShapeDtypeStruct((blocks, rows, 4 * head_dim), jnp.bfloat16),
        scratch_shapes=[
            pltpu.VMEM(queries.shape, jnp.bfloat16),
            pltpu.VMEM(cached_key_rows.shape, jnp.bfloat16),
            pltpu.VMEM(cached_value_rows.shape, jnp.bfloat16),
            pltpu.VMEM((pairs, group_rows, cache_len), jnp.float32),
            pltpu.VMEM((pairs, group_rows, cache_len), jnp.bfloat16),
            pltpu.VMEM((pairs, group_rows, head_dim), jnp.float32),
            pltpu.SemaphoreType.DMA,
            pltpu.SemaphoreType.DMA((requests,)),
            pltpu.SemaphoreType.DMA((requests,)),
        ],
        compiler_params=pltpu.CompilerParams(vmem_limit_bytes=60 * 1024 * 1024),
        cost_estimate=pl.CostEstimate(
            flops=4 * rows * heads * cache_len * head_dim,
            bytes_accessed=2 * 2 * cached_key_rows.size,
            transcendentals=rows * heads * cache_len,
        ),
        name="attend",
    )(cache_fill_length, queries, cached_key_rows, cached_value_rows)


def cut_kernel(wo_ref, out_ref, sems):
    bands, depth, band = out_ref.shape
    low = 1 - lax.rem(lax.axis_index("tensor") // SIDE, 2)
    row = pl.multiple_of(lax.rem(lax.axis_index("dp"), 2) * depth, depth)
    copies = [
        pltpu.make_async_copy(
            wo_ref.at[pl.ds(row, depth), pl.ds(pl.multiple_of((2 * high + low) * band, band), band)],
            out_ref.at[high],
            sems.at[high],
        )
        for high in range(bands)
    ]
    for copy in copies:
        copy.start()
    for copy in copies:
        copy.wait()


def cut_wo(wo):
    bands = SIDE // 2
    return pl.pallas_call(
        cut_kernel,
        in_specs=[pl.BlockSpec(memory_space=pltpu.HBM)],
        out_specs=pl.BlockSpec(memory_space=pltpu.VMEM),
        out_shape=jax.ShapeDtypeStruct((bands, wo.shape[0] // 2, wo.shape[1] // SIDE), wo.dtype),
        scratch_shapes=[pltpu.SemaphoreType.DMA((bands,))],
        cost_estimate=pl.CostEstimate(flops=0, bytes_accessed=2 * wo.size, transcendentals=0),
        name="cut_wo",
    )(wo)


def project_kernel(rows_ref, own_ref, mine_ref, sibling_ref, *out_refs):
    tensor = lax.axis_index("tensor")
    y, x = tensor // SIDE, lax.rem(tensor, SIDE)
    core = lax.rem(lax.axis_index("dp"), 2)
    half = mine_ref.shape[1]
    width = rows_ref.shape[1] // 2
    own_rows = rows_ref[:, :width]
    mine_rows = rows_ref[:, pl.ds(pl.multiple_of(width + core * half, half), half)]
    sibling_rows = rows_ref[:, pl.ds(pl.multiple_of(width + (1 - core) * half, half), half)]
    for s, out_ref in enumerate(out_refs):
        across = lax.rem(x + s, SIDE)
        for v in range(2):
            line = y ^ (2 * v)
            own_at = pl.multiple_of((line * SIDE + across) * width, width)
            at = pl.ds(pl.multiple_of(across * width, width), width)
            part = jnp.dot(
                own_rows, own_ref[:, pl.ds(own_at, width)], preferred_element_type=jnp.float32
            )
            part += jnp.dot(
                mine_rows, mine_ref[line // 2, :, at], preferred_element_type=jnp.float32
            )
            part += jnp.dot(
                sibling_rows, sibling_ref[line // 2, :, at], preferred_element_type=jnp.float32
            )
            out_ref[v] = part.astype(out_ref.dtype)


def project(head_rows, wo, mine, sibling):
    rows, depth = head_rows.shape
    width = wo.shape[1] // (SIDE * SIDE)
    resident = pl.BlockSpec(memory_space=pltpu.VMEM)
    kinds = [jnp.float32] + [jnp.bfloat16] * (SIDE - 1)
    return pl.pallas_call(
        project_kernel,
        in_specs=[resident] * 4,
        out_specs=[resident for _ in kinds],
        out_shape=[jax.ShapeDtypeStruct((2, rows, width), kind) for kind in kinds],
        compiler_params=pltpu.CompilerParams(vmem_limit_bytes=24 * 1024 * 1024),
        cost_estimate=pl.CostEstimate(
            flops=rows * depth * wo.shape[1],
            bytes_accessed=3 * wo.size + rows * wo.shape[1],
            transcendentals=0,
        ),
        name="project",
    )(head_rows, wo, mine, sibling)


def down_kernel(owned_ref, down_ref, out_ref, ids_ref):
    rows, columns = owned_ref.shape[0], down_ref.shape[1]
    rank = out_ref.shape[1]
    adapters = down_ref.shape[0] // rank
    every = lax.dot_general(
        down_ref[...],
        owned_ref[:, :columns],
        (((1,), (1,)), ((), ())),
        preferred_element_type=jnp.float32,
    )
    ids = jnp.transpose(owned_ref[:, columns:].astype(jnp.float32))[:8]
    ids_ref[...] = ids
    adapter = lax.broadcasted_iota(jnp.int32, (adapters, rank, rows), 0).astype(jnp.float32)
    chosen = adapter == ids[:1].reshape(1, 1, rows)
    part = jnp.sum(jnp.where(chosen, every.reshape(adapters, rank, rows), 0.0), axis=0)
    for copy in range(out_ref.shape[0]):
        out_ref[copy] = part


def shrink_down(owned, down, shares, rank):
    rows = owned.shape[0]
    resident = pl.BlockSpec(memory_space=pltpu.VMEM)
    return pl.pallas_call(
        down_kernel,
        in_specs=[resident] * 2,
        out_specs=[resident] * 2,
        out_shape=[
            jax.ShapeDtypeStruct((shares, rank, rows), jnp.float32),
            jax.ShapeDtypeStruct((8, rows), jnp.float32),
        ],
        compiler_params=pltpu.CompilerParams(vmem_limit_bytes=16 * 1024 * 1024),
        cost_estimate=pl.CostEstimate(
            flops=2 * rows * down.size, bytes_accessed=4 * down.size, transcendentals=0
        ),
        name="shrink_down",
    )(owned, down)


def up_kernel(partials_ref, ids_ref, up_ref, out_ref):
    shares, rank, rows = partials_ref.shape
    adapters = up_ref.shape[0] // rank
    shrink = partials_ref[0]
    for share in range(1, shares):
        shrink += partials_ref[share]
    shrink = shrink.astype(jnp.bfloat16).astype(jnp.float32)
    adapter = lax.broadcasted_iota(jnp.int32, (adapters, rank, rows), 0).astype(jnp.float32)
    chosen = adapter == ids_ref[:1].reshape(1, 1, rows)
    spread = jnp.where(chosen, shrink.reshape(1, rank, rows), 0.0)
    out_ref[...] = lax.dot_general(
        spread.reshape(adapters * rank, rows).astype(jnp.bfloat16),
        up_ref[...],
        (((0,), (0,)), ((), ())),
        preferred_element_type=jnp.float32,
    ).astype(jnp.bfloat16)


def expand_up(partials, ids, up):
    rows = partials.shape[2]
    resident = pl.BlockSpec(memory_space=pltpu.VMEM)
    return pl.pallas_call(
        up_kernel,
        in_specs=[resident] * 3,
        out_specs=resident,
        out_shape=jax.ShapeDtypeStruct((rows, up.shape[1]), jnp.bfloat16),
        compiler_params=pltpu.CompilerParams(vmem_limit_bytes=16 * 1024 * 1024),
        cost_estimate=pl.CostEstimate(
            flops=2 * rows * up.size, bytes_accessed=4 * up.size, transcendentals=0
        ),
        name="expand_up",
    )(partials, ids, up)


def shift_pairs(value, target):
    pairs = []
    for y in range(SIDE):
        for x in range(SIDE):
            to_y, to_x = target(y, x)
            pairs.append((y * SIDE + x, to_y * SIDE + to_x))
    return lax.ppermute(value, "tensor", pairs)


def after(value, *earlier):
    return lax.optimization_barrier((value,) + earlier)[0]


def on_device(
    queries,
    cached_key_rows,
    cached_value_rows,
    cache_fill_length,
    request_adapters,
    wo,
    adapter_down_weight,
    adapter_up_weight,
):
    owners = lax.axis_size("dp")
    shares = lax.axis_size("tensor")
    group_size = request_adapters.shape[0]
    owner_partial, rank, width = adapter_down_weight.shape
    capacity = group_size // owners
    steps = queries.shape[1]
    rows = group_size * steps

    owner_ids = request_adapters // owner_partial
    local_ids = request_adapters % owner_partial
    order = jnp.arange(group_size, dtype=jnp.int32)
    earlier = (owner_ids[:, None] == owner_ids[None, :]) & (order[:, None] > order[None, :])
    slots = owner_ids * capacity + jnp.sum(earlier.astype(jnp.int32), axis=1)
    row_slots = (slots[:, None] * steps + jnp.arange(steps, dtype=jnp.int32)).reshape(rows)
    to_slots = (jnp.arange(rows, dtype=jnp.int32)[:, None] == row_slots[None, :]).astype(
        jnp.bfloat16
    )
    row_locals = jnp.repeat(local_ids, steps).astype(jnp.bfloat16)
    id_lanes = jnp.broadcast_to(row_locals[:, None], (rows, 128))

    mine = shift_pairs(cut_wo(wo), lambda y, x: (y ^ 1, x))
    sibling = lax.ppermute(mine, "dp", [(d, d ^ 1) for d in range(owners)])

    attended = attend(queries, cached_key_rows, cached_value_rows, cache_fill_length)
    pair_rows = lax.all_to_all(attended, "tensor", 0, 0, tiled=True).reshape(rows, 2 * width)
    head_rows = pair_rows[:, :width]

    payload = jnp.dot(
        to_slots,
        jnp.concatenate([head_rows, id_lanes], axis=1),
        preferred_element_type=jnp.float32,
    ).astype(jnp.bfloat16)
    own, *others = project(after(pair_rows, payload), wo, mine, sibling)
    arrived = [
        shift_pairs(part, lambda y, x, s=s: (y, (x + s) % SIDE))
        for s, part in enumerate(others, start=1)
    ]
    owned = lax.all_to_all(
        payload.reshape(owners, capacity * steps, width + 128), "dp", 0, 0, tiled=True
    ).reshape(rows, width + 128)
    partial_shrink, ids = shrink_down(
        after(owned, own), adapter_down_weight.reshape(owner_partial * rank, width), shares, rank
    )
    partials = lax.all_to_all(partial_shrink, "tensor", 0, 0, tiled=True)
    delta = expand_up(partials, ids, adapter_up_weight.reshape(owner_partial * rank, width))
    along_x = [own[v] + sum(part[v].astype(jnp.float32) for part in arrived) for v in range(2)]
    delta = after(delta, *along_x)
    returned = lax.all_to_all(
        delta.reshape(owners, capacity * steps, width), "dp", 0, 0, tiled=True
    ).reshape(rows, width)

    across_y = shift_pairs(along_x[1].astype(jnp.bfloat16), lambda y, x: (y ^ 2, x))
    base_output = along_x[0] + across_y.astype(jnp.float32)
    adapter_delta = jnp.einsum(
        "sq,sd->qd", to_slots, returned, preferred_element_type=jnp.float32
    )
    return (base_output + adapter_delta).astype(jnp.bfloat16).reshape(group_size, steps, width)


def solution(mesh):
    in_specs = (
        P(("dp", "tensor"), None, None, None),
        P(("dp", "tensor"), None, None, None),
        P(("dp", "tensor"), None, None, None),
        P(("dp", "tensor")),
        P("dp"),
        P("tensor", None),
        P("dp", None, "tensor"),
        P("dp", None, "tensor"),
    )
    out_specs = P("dp", None, "tensor")
    return jax.shard_map(
        on_device, mesh=mesh, in_specs=in_specs, out_specs=out_specs, check_vma=False
    )
```

```python
import math

import jax
import jax.numpy as jnp
from jax import lax
from jax.experimental import pallas as pl
from jax.experimental.pallas import tpu as pltpu
from jax.sharding import PartitionSpec as P

NEG_FILL = -1e30
SIDE = 4


def torus_place():
    tensor = lax.axis_index("tensor")
    y, x = tensor // SIDE, lax.rem(tensor, SIDE)
    odd = lax.rem(lax.axis_index("dp"), 2)
    pair, line = y + odd * (x - y), x + odd * (y - x)
    pair_stride = SIDE + odd * (1 - SIDE)
    return pair, line, pair_stride, SIDE + 1 - pair_stride


def attend_kernel(
    fill_ref, queries_ref, keys_ref, values_ref, out_ref,
    query_buf, key_buf, value_buf, score_buf, weight_buf, grouped_buf,
    query_sem, key_sem, value_sem,
):
    requests, steps, heads, head_dim = query_buf.shape
    kv_heads, cache_len = key_buf.shape[1], key_buf.shape[2]
    per_group = heads // kv_heads
    group_rows = steps * per_group
    query_copy = pltpu.make_async_copy(queries_ref, query_buf, query_sem)
    key_copies = [
        pltpu.make_async_copy(keys_ref.at[r], key_buf.at[r], key_sem.at[r]) for r in range(requests)
    ]
    value_copies = [
        pltpu.make_async_copy(values_ref.at[r], value_buf.at[r], value_sem.at[r])
        for r in range(requests)
    ]
    query_copy.start()
    for copy in key_copies:
        copy.start()
    position = lax.broadcasted_iota(jnp.int32, (group_rows, cache_len), 1)
    step_of = lax.broadcasted_iota(jnp.int32, (group_rows, cache_len), 0) // per_group
    reach = position + steps - step_of
    query_copy.wait()
    for r in range(requests):
        every = query_buf[r].astype(jnp.float32)
        key_copies[r].wait()
        value_copies[r].start()
        for k in range(kv_heads):
            grouped = every[:, k * per_group : (k + 1) * per_group, :]
            grouped = grouped.reshape(group_rows, head_dim).astype(jnp.bfloat16)
            score_buf[r * kv_heads + k] = lax.dot_general(
                grouped,
                key_buf[r, k],
                (((1,), (1,)), ((), ())),
                preferred_element_type=jnp.float32,
            )
    for r in range(requests):
        valid = reach <= fill_ref[r]
        for k in range(kv_heads):
            scores = score_buf[r * kv_heads + k] * (1.0 / math.sqrt(head_dim))
            scores = jnp.where(valid, scores, NEG_FILL)
            raised = jnp.exp(scores - jnp.max(scores, axis=1, keepdims=True))
            weights = raised * (1.0 / jnp.sum(raised, axis=1, keepdims=True))
            weight_buf[r * kv_heads + k] = weights.astype(jnp.bfloat16)
    for r in range(requests):
        value_copies[r].wait()
        for k in range(kv_heads):
            grouped_buf[k, r * group_rows : (r + 1) * group_rows] = jnp.dot(
                weight_buf[r * kv_heads + k], value_buf[r, k], preferred_element_type=jnp.float32
            ).astype(jnp.bfloat16)
    every_rows = requests * group_rows
    rows = requests * steps
    old = lax.broadcasted_iota(jnp.int32, (every_rows, every_rows), 1)
    new = lax.broadcasted_iota(jnp.int32, (every_rows, every_rows), 0)
    turn = (old == new % rows * per_group + new // rows).astype(jnp.bfloat16)
    for k in range(kv_heads):
        turned = jnp.dot(turn, grouped_buf[k], preferred_element_type=jnp.float32)
        turned = turned.astype(jnp.bfloat16)
        for g in range(per_group):
            block, at = k * (per_group // 2) + g // 2, g % 2 * head_dim
            piece = turned[g * rows : (g + 1) * rows]
            out_ref[block, :, at : at + head_dim] = piece


def attend(queries, cached_key_rows, cached_value_rows, cache_fill_length):
    requests, steps, heads, head_dim = queries.shape
    kv_heads, cache_len = cached_key_rows.shape[1:3]
    blocks, rows = heads // 2, requests * steps
    pairs, group_rows = requests * kv_heads, steps * heads // kv_heads
    distant = pl.BlockSpec(memory_space=pl.ANY)
    return pl.pallas_call(
        attend_kernel,
        in_specs=[pl.BlockSpec(memory_space=pltpu.SMEM)] + [distant] * 3,
        out_specs=pl.BlockSpec(memory_space=pltpu.VMEM),
        out_shape=jax.ShapeDtypeStruct((blocks, rows, 2 * head_dim), jnp.bfloat16),
        scratch_shapes=[
            pltpu.VMEM(queries.shape, jnp.bfloat16),
            pltpu.VMEM(cached_key_rows.shape, jnp.bfloat16),
            pltpu.VMEM(cached_value_rows.shape, jnp.bfloat16),
            pltpu.VMEM((pairs, group_rows, cache_len), jnp.float32),
            pltpu.VMEM((pairs, group_rows, cache_len), jnp.bfloat16),
            pltpu.VMEM((kv_heads, requests * group_rows, head_dim), jnp.bfloat16),
            pltpu.SemaphoreType.DMA,
            pltpu.SemaphoreType.DMA((requests,)),
            pltpu.SemaphoreType.DMA((requests,)),
        ],
        compiler_params=pltpu.CompilerParams(vmem_limit_bytes=60 * 1024 * 1024),
        cost_estimate=pl.CostEstimate(
            flops=4 * rows * heads * cache_len * head_dim,
            bytes_accessed=2 * 2 * cached_key_rows.size,
            transcendentals=rows * heads * cache_len,
        ),
        name="attend",
    )(cache_fill_length, queries, cached_key_rows, cached_value_rows)


def payload_kernel(rows_ref, slots_ref, locals_ref, out_ref):
    rows, width = rows_ref.shape
    slot = lax.broadcasted_iota(jnp.int32, (rows, rows), 0)
    hit = slot == slots_ref[...]
    out_ref[:, :width] = jnp.dot(
        hit.astype(jnp.bfloat16), rows_ref[...], preferred_element_type=jnp.float32
    ).astype(jnp.bfloat16)
    ids = jnp.sum(jnp.where(hit, locals_ref[...].astype(jnp.float32), 0.0), axis=1, keepdims=True)
    out_ref[:, width:] = jnp.broadcast_to(ids, (rows, out_ref.shape[1] - width)).astype(jnp.bfloat16)


def make_payload(head_rows, row_slots, row_locals):
    rows, width = head_rows.shape
    resident = pl.BlockSpec(memory_space=pltpu.VMEM)
    return pl.pallas_call(
        payload_kernel,
        in_specs=[resident] * 3,
        out_specs=resident,
        out_shape=jax.ShapeDtypeStruct((rows, width + 128), jnp.bfloat16),
        compiler_params=pltpu.CompilerParams(vmem_limit_bytes=16 * 1024 * 1024),
        cost_estimate=pl.CostEstimate(
            flops=2 * rows * rows * width, bytes_accessed=8 * rows * width, transcendentals=0
        ),
        name="make_payload",
    )(head_rows, row_slots, row_locals)


def project_kernel(rows_ref, wo_ref, *refs):
    out_refs, wo_buf, wo_sem = refs[:SIDE], refs[SIDE], refs[SIDE + 1]
    pair, line, pair_stride, line_stride = torus_place()
    width = wo_buf.shape[2]
    blocks = [(s, u) for s in (2, 1, 3, 0) for u in range(SIDE)]
    copies = []
    for i, (s, u) in enumerate(blocks):
        along, across = lax.rem(line + s, SIDE), lax.rem(pair + u, SIDE)
        at = pl.multiple_of((across * pair_stride + along * line_stride) * width, width)
        copies.append(
            pltpu.make_async_copy(wo_ref.at[:, pl.ds(at, width)], wo_buf.at[i], wo_sem.at[i])
        )
    for copy in copies:
        copy.start()
    for i, (s, u) in enumerate(blocks):
        copies[i].wait()
        part = jnp.dot(rows_ref[...], wo_buf[i], preferred_element_type=jnp.float32)
        out_refs[s][u] = part.astype(out_refs[s].dtype)


def project(head_rows, wo):
    rows, depth = head_rows.shape
    width = wo.shape[1] // (SIDE * SIDE)
    resident = pl.BlockSpec(memory_space=pltpu.VMEM)
    kinds = [jnp.float32] + [jnp.bfloat16] * (SIDE - 1)
    return pl.pallas_call(
        project_kernel,
        in_specs=[resident, pl.BlockSpec(memory_space=pl.ANY)],
        out_specs=[resident for _ in kinds],
        out_shape=[jax.ShapeDtypeStruct((SIDE, rows, width), kind) for kind in kinds],
        scratch_shapes=[
            pltpu.VMEM((SIDE * SIDE, depth, width), wo.dtype),
            pltpu.SemaphoreType.DMA((SIDE * SIDE,)),
        ],
        compiler_params=pltpu.CompilerParams(vmem_limit_bytes=24 * 1024 * 1024),
        cost_estimate=pl.CostEstimate(
            flops=2 * rows * depth * wo.shape[1],
            bytes_accessed=2 * wo.size + 3 * rows * wo.shape[1],
            transcendentals=0,
        ),
        name="project",
    )(head_rows, pltpu.with_memory_space_constraint(wo, pltpu.HBM))


def down_kernel(owned_ref, down_ref, out_ref, ids_ref, down_buf, down_sem):
    copy_down = pltpu.make_async_copy(down_ref, down_buf, down_sem)
    copy_down.start()
    rows, columns = owned_ref.shape[0], down_ref.shape[1]
    rank = out_ref.shape[1]
    adapters = down_ref.shape[0] // rank
    ids = jnp.transpose(owned_ref[:, columns:].astype(jnp.float32))[:8]
    ids_ref[...] = ids
    copy_down.wait()
    every = lax.dot_general(
        down_buf[...],
        owned_ref[:, :columns],
        (((1,), (1,)), ((), ())),
        preferred_element_type=jnp.float32,
    )
    adapter = lax.broadcasted_iota(jnp.int32, (adapters, rank, rows), 0).astype(jnp.float32)
    chosen = adapter == ids[:1].reshape(1, 1, rows)
    part = jnp.sum(jnp.where(chosen, every.reshape(adapters, rank, rows), 0.0), axis=0)
    for share in range(out_ref.shape[0]):
        out_ref[share] = part


def shrink_down(owned, down, shares, rank):
    rows = owned.shape[0]
    resident = pl.BlockSpec(memory_space=pltpu.VMEM)
    return pl.pallas_call(
        down_kernel,
        in_specs=[resident, pl.BlockSpec(memory_space=pl.ANY)],
        out_specs=[resident] * 2,
        scratch_shapes=[pltpu.VMEM(down.shape, down.dtype), pltpu.SemaphoreType.DMA],
        out_shape=[
            jax.ShapeDtypeStruct((shares, rank, rows), jnp.float32),
            jax.ShapeDtypeStruct((8, rows), jnp.float32),
        ],
        compiler_params=pltpu.CompilerParams(vmem_limit_bytes=16 * 1024 * 1024),
        cost_estimate=pl.CostEstimate(
            flops=2 * rows * down.size, bytes_accessed=4 * down.size, transcendentals=0
        ),
        name="shrink_down",
    )(owned, pltpu.with_memory_space_constraint(down, pltpu.HBM))


def up_kernel(partials_ref, ids_ref, up_ref, out_ref, up_buf, up_sem):
    copy_up = pltpu.make_async_copy(up_ref, up_buf, up_sem)
    copy_up.start()
    shares, rank, rows = partials_ref.shape
    adapters = up_ref.shape[0] // rank
    shrink = partials_ref[0]
    for share in range(1, shares):
        shrink += partials_ref[share]
    shrink = shrink.astype(jnp.bfloat16).astype(jnp.float32)
    adapter = lax.broadcasted_iota(jnp.int32, (adapters, rank, rows), 0).astype(jnp.float32)
    chosen = adapter == ids_ref[:1].reshape(1, 1, rows)
    spread = jnp.where(chosen, shrink.reshape(1, rank, rows), 0.0)
    copy_up.wait()
    out_ref[...] = lax.dot_general(
        spread.reshape(adapters * rank, rows).astype(jnp.bfloat16),
        up_buf[...],
        (((0,), (0,)), ((), ())),
        preferred_element_type=jnp.float32,
    ).astype(jnp.bfloat16)


def expand_up(partials, ids, up):
    rows = partials.shape[2]
    resident = pl.BlockSpec(memory_space=pltpu.VMEM)
    return pl.pallas_call(
        up_kernel,
        in_specs=[resident, resident, pl.BlockSpec(memory_space=pl.ANY)],
        out_specs=resident,
        scratch_shapes=[pltpu.VMEM(up.shape, up.dtype), pltpu.SemaphoreType.DMA],
        out_shape=jax.ShapeDtypeStruct((rows, up.shape[1]), jnp.bfloat16),
        compiler_params=pltpu.CompilerParams(vmem_limit_bytes=16 * 1024 * 1024),
        cost_estimate=pl.CostEstimate(
            flops=2 * rows * up.size, bytes_accessed=4 * up.size, transcendentals=0
        ),
        name="expand_up",
    )(partials, ids, pltpu.with_memory_space_constraint(up, pltpu.HBM))


def finish_kernel(slots_ref, returned_ref, base_ref, *refs):
    across_refs, out_ref = refs[:-1], refs[-1]
    rows = returned_ref.shape[0]
    slot = lax.broadcasted_iota(jnp.int32, (rows, rows), 0)
    to_slots = (slot == slots_ref[...]).astype(jnp.bfloat16)
    delta = lax.dot_general(
        to_slots, returned_ref[...], (((0,), (0,)), ((), ())), preferred_element_type=jnp.float32
    )
    total = base_ref[...] + delta
    for across_ref in across_refs:
        total += across_ref[...].astype(jnp.float32)
    out_ref[...] = total.reshape(out_ref.shape).astype(out_ref.dtype)


def finish(row_slots, returned, base, across, out_shape):
    resident = pl.BlockSpec(memory_space=pltpu.VMEM)
    return pl.pallas_call(
        finish_kernel,
        in_specs=[resident] * (3 + len(across)),
        out_specs=resident,
        out_shape=jax.ShapeDtypeStruct(out_shape, jnp.bfloat16),
        compiler_params=pltpu.CompilerParams(vmem_limit_bytes=16 * 1024 * 1024),
        cost_estimate=pl.CostEstimate(
            flops=2 * returned.size * returned.shape[0],
            bytes_accessed=8 * returned.size,
            transcendentals=0,
        ),
        name="finish",
    )(row_slots, returned, base, *across)


def move(value, owners, target):
    pairs = []
    for d in range(owners):
        for pair in range(SIDE):
            for line in range(SIDE):
                to_pair, to_line = target(pair, line)
                if d % 2 == 0:
                    here, there = pair * SIDE + line, to_pair * SIDE + to_line
                else:
                    here, there = line * SIDE + pair, to_line * SIDE + to_pair
                pairs.append((d * SIDE * SIDE + here, d * SIDE * SIDE + there))
    return lax.ppermute(value, ("dp", "tensor"), pairs)


def after(value, *earlier):
    return lax.optimization_barrier((value,) + earlier)[0]


def on_device(
    queries,
    cached_key_rows,
    cached_value_rows,
    cache_fill_length,
    request_adapters,
    wo,
    adapter_down_weight,
    adapter_up_weight,
):
    owners = lax.axis_size("dp")
    shares = lax.axis_size("tensor")
    group_size = request_adapters.shape[0]
    owner_partial, rank, width = adapter_down_weight.shape
    capacity = group_size // owners
    steps = queries.shape[1]
    rows = group_size * steps

    owner_ids = request_adapters // owner_partial
    local_ids = request_adapters % owner_partial
    order = jnp.arange(group_size, dtype=jnp.int32)
    earlier = (owner_ids[:, None] == owner_ids[None, :]) & (order[:, None] > order[None, :])
    slots = owner_ids * capacity + jnp.sum(earlier.astype(jnp.int32), axis=1)
    row_slots = (slots[:, None] * steps + jnp.arange(steps, dtype=jnp.int32)).reshape(1, rows)
    row_locals = jnp.repeat(local_ids, steps)[None, :]

    attended = attend(queries, cached_key_rows, cached_value_rows, cache_fill_length)
    head_rows = lax.all_to_all(attended, "tensor", 0, 0, tiled=True).reshape(rows, width)

    payload = make_payload(head_rows, row_slots, row_locals)
    own, *others = project(after(head_rows, payload), wo)
    arrived = [
        move(part, owners, lambda pair, line, s=s: (pair, (line + s) % SIDE))
        for s, part in enumerate(others, start=1)
    ]
    owned = lax.all_to_all(
        payload.reshape(owners, capacity * steps, width + 128), "dp", 0, 0, tiled=True
    ).reshape(rows, width + 128)
    partial_shrink, ids = shrink_down(
        after(owned, own), adapter_down_weight.reshape(owner_partial * rank, width), shares, rank
    )
    partials = lax.all_to_all(partial_shrink, "tensor", 0, 0, tiled=True)
    delta = expand_up(partials, ids, adapter_up_weight.reshape(owner_partial * rank, width))
    returned = lax.all_to_all(
        delta.reshape(owners, capacity * steps, width), "dp", 0, 0, tiled=True
    ).reshape(rows, width)

    along_line = [
        own[u] + sum(part[u].astype(jnp.float32) for part in arrived) for u in range(SIDE)
    ]
    across = [
        move(
            along_line[u].astype(jnp.bfloat16),
            owners,
            lambda pair, line, u=u: ((pair + u) % SIDE, line),
        )
        for u in range(1, SIDE)
    ]
    return finish(
        row_slots, returned, along_line[0], across, (group_size, steps, width)
    )


def solution(mesh):
    in_specs = (
        P(("dp", "tensor"), None, None, None),
        P(("dp", "tensor"), None, None, None),
        P(("dp", "tensor"), None, None, None),
        P(("dp", "tensor")),
        P("dp"),
        P("tensor", None),
        P("dp", None, "tensor"),
        P("dp", None, "tensor"),
    )
    out_specs = P("dp", None, "tensor")
    return jax.shard_map(
        on_device, mesh=mesh, in_specs=in_specs, out_specs=out_specs, check_vma=False
    )
```

```python
import math

import jax
import jax.numpy as jnp
from jax import lax
from jax.experimental import pallas as pl
from jax.experimental.pallas import tpu as pltpu
from jax.sharding import PartitionSpec as P

NEG_FILL = -1e30
FAR_FLOPS = 20_000_000_000
SIDE = 4


def torus_place():
    tensor = lax.axis_index("tensor")
    y, x = tensor // SIDE, lax.rem(tensor, SIDE)
    odd = lax.rem(lax.axis_index("dp"), 2)
    pair, line = y + odd * (x - y), x + odd * (y - x)
    pair_stride = SIDE + odd * (1 - SIDE)
    return pair, line, pair_stride, SIDE + 1 - pair_stride


def attend_kernel(
    fill_ref, queries_ref, keys_ref, values_ref, out_ref,
    query_buf, key_buf, value_buf, score_buf, weight_buf, grouped_buf,
    query_sem, key_sem, value_sem,
):
    requests, steps, heads, head_dim = query_buf.shape
    kv_heads, cache_len = key_buf.shape[1], key_buf.shape[2]
    per_group = heads // kv_heads
    group_rows = steps * per_group
    query_copy = pltpu.make_async_copy(queries_ref, query_buf, query_sem)
    key_copies = [
        pltpu.make_async_copy(keys_ref.at[r], key_buf.at[r], key_sem.at[r]) for r in range(requests)
    ]
    value_copies = [
        pltpu.make_async_copy(values_ref.at[r], value_buf.at[r], value_sem.at[r])
        for r in range(requests)
    ]
    query_copy.start()
    for copy in key_copies:
        copy.start()
    position = lax.broadcasted_iota(jnp.int32, (group_rows, cache_len), 1)
    step_of = lax.broadcasted_iota(jnp.int32, (group_rows, cache_len), 0) // per_group
    reach = position + steps - step_of
    query_copy.wait()
    for r in range(requests):
        every = query_buf[r].astype(jnp.float32)
        key_copies[r].wait()
        value_copies[r].start()
        for k in range(kv_heads):
            grouped = every[:, k * per_group : (k + 1) * per_group, :]
            grouped = grouped.reshape(group_rows, head_dim).astype(jnp.bfloat16)
            score_buf[r * kv_heads + k] = lax.dot_general(
                grouped,
                key_buf[r, k],
                (((1,), (1,)), ((), ())),
                preferred_element_type=jnp.float32,
            )
    for r in range(requests):
        valid = reach <= fill_ref[r]
        for k in range(kv_heads):
            scores = score_buf[r * kv_heads + k] * (1.0 / math.sqrt(head_dim))
            scores = jnp.where(valid, scores, NEG_FILL)
            raised = jnp.exp(scores - jnp.max(scores, axis=1, keepdims=True))
            weights = raised * (1.0 / jnp.sum(raised, axis=1, keepdims=True))
            weight_buf[r * kv_heads + k] = weights.astype(jnp.bfloat16)
    for r in range(requests):
        value_copies[r].wait()
        for k in range(kv_heads):
            grouped_buf[k, r * group_rows : (r + 1) * group_rows] = jnp.dot(
                weight_buf[r * kv_heads + k], value_buf[r, k], preferred_element_type=jnp.float32
            ).astype(jnp.bfloat16)
    every_rows = requests * group_rows
    rows = requests * steps
    old = lax.broadcasted_iota(jnp.int32, (every_rows, every_rows), 1)
    new = lax.broadcasted_iota(jnp.int32, (every_rows, every_rows), 0)
    turn = (old == new % rows * per_group + new // rows).astype(jnp.bfloat16)
    for k in range(kv_heads):
        turned = jnp.dot(turn, grouped_buf[k], preferred_element_type=jnp.float32)
        turned = turned.astype(jnp.bfloat16)
        for g in range(per_group):
            block, at = k * (per_group // 2) + g // 2, g % 2 * head_dim
            piece = turned[g * rows : (g + 1) * rows]
            out_ref[block, :, at : at + head_dim] = piece


def attend(queries, cached_key_rows, cached_value_rows, cache_fill_length):
    requests, steps, heads, head_dim = queries.shape
    kv_heads, cache_len = cached_key_rows.shape[1:3]
    blocks, rows = heads // 2, requests * steps
    pairs, group_rows = requests * kv_heads, steps * heads // kv_heads
    distant = pl.BlockSpec(memory_space=pl.ANY)
    return pl.pallas_call(
        attend_kernel,
        in_specs=[pl.BlockSpec(memory_space=pltpu.SMEM)] + [distant] * 3,
        out_specs=pl.BlockSpec(memory_space=pltpu.VMEM),
        out_shape=jax.ShapeDtypeStruct((blocks, rows, 2 * head_dim), jnp.bfloat16),
        scratch_shapes=[
            pltpu.VMEM(queries.shape, jnp.bfloat16),
            pltpu.VMEM(cached_key_rows.shape, jnp.bfloat16),
            pltpu.VMEM(cached_value_rows.shape, jnp.bfloat16),
            pltpu.VMEM((pairs, group_rows, cache_len), jnp.float32),
            pltpu.VMEM((pairs, group_rows, cache_len), jnp.bfloat16),
            pltpu.VMEM((kv_heads, requests * group_rows, head_dim), jnp.bfloat16),
            pltpu.SemaphoreType.DMA,
            pltpu.SemaphoreType.DMA((requests,)),
            pltpu.SemaphoreType.DMA((requests,)),
        ],
        compiler_params=pltpu.CompilerParams(vmem_limit_bytes=60 * 1024 * 1024),
        cost_estimate=pl.CostEstimate(
            flops=4 * rows * heads * cache_len * head_dim,
            bytes_accessed=2 * 2 * cached_key_rows.size,
            transcendentals=rows * heads * cache_len,
        ),
        name="attend",
    )(cache_fill_length, queries, cached_key_rows, cached_value_rows)


def payload_kernel(rows_ref, slots_ref, locals_ref, out_ref):
    rows, width = rows_ref.shape
    slot = lax.broadcasted_iota(jnp.int32, (rows, rows), 0)
    hit = (slot == slots_ref[...]).astype(jnp.bfloat16)
    out_ref[:, :width] = jnp.dot(
        hit, rows_ref[...], preferred_element_type=jnp.float32
    ).astype(jnp.bfloat16)
    ids = locals_ref[...].astype(jnp.float32).astype(jnp.bfloat16)
    out_ref[:, width:] = lax.dot_general(
        hit,
        jnp.broadcast_to(ids, (out_ref.shape[1] - width, rows)),
        (((1,), (1,)), ((), ())),
        preferred_element_type=jnp.float32,
    ).astype(jnp.bfloat16)


def make_payload(head_rows, row_slots, row_locals):
    rows, width = head_rows.shape
    resident = pl.BlockSpec(memory_space=pltpu.VMEM)
    return pl.pallas_call(
        payload_kernel,
        in_specs=[resident] * 3,
        out_specs=resident,
        out_shape=jax.ShapeDtypeStruct((rows, width + 128), jnp.bfloat16),
        compiler_params=pltpu.CompilerParams(vmem_limit_bytes=16 * 1024 * 1024),
        cost_estimate=pl.CostEstimate(
            flops=2 * rows * rows * width, bytes_accessed=8 * rows * width, transcendentals=0
        ),
        name="make_payload",
    )(head_rows, row_slots, row_locals)


def project_kernel(rows_ref, wo_ref, *refs):
    own_ref, own_buf, own_sem = refs[0], refs[SIDE], refs[SIDE + 1]
    out_refs = (own_buf,) + refs[1:SIDE]
    pair, line, pair_stride, line_stride = torus_place()
    width = rows_ref.shape[1]
    for s, out_ref in enumerate(out_refs):
        along = lax.rem(line + s, SIDE)
        for u in range(SIDE):
            across = lax.rem(pair + u, SIDE)
            at = pl.multiple_of((across * pair_stride + along * line_stride) * width, width)
            part = jnp.dot(
                rows_ref[...], wo_ref[:, pl.ds(at, width)], preferred_element_type=jnp.float32
            )
            out_ref[u] = part.astype(out_ref.dtype)
        if s == 0:
            own_copy = pltpu.make_async_copy(own_buf, own_ref, own_sem)
            own_copy.start()
    own_copy.wait()


def project(head_rows, wo):
    rows, depth = head_rows.shape
    width = wo.shape[1] // (SIDE * SIDE)
    resident = pl.BlockSpec(memory_space=pltpu.VMEM)
    return pl.pallas_call(
        project_kernel,
        in_specs=[resident] * 2,
        out_specs=[pl.BlockSpec(memory_space=pltpu.HBM)] + [resident] * (SIDE - 1),
        out_shape=[pltpu.HBM((SIDE, rows, width), jnp.float32)]
        + [jax.ShapeDtypeStruct((SIDE, rows, width), jnp.bfloat16)] * (SIDE - 1),
        scratch_shapes=[pltpu.VMEM((SIDE, rows, width), jnp.float32), pltpu.SemaphoreType.DMA],
        compiler_params=pltpu.CompilerParams(vmem_limit_bytes=16 * 1024 * 1024),
        cost_estimate=pl.CostEstimate(
            flops=2 * rows * depth * wo.shape[1],
            bytes_accessed=2 * wo.size + 3 * rows * wo.shape[1],
            transcendentals=0,
        ),
        name="project",
    )(head_rows, wo)


def down_kernel(owned_ref, down_ref, up_ref, out_ref, ids_ref):
    del up_ref
    rows, columns = owned_ref.shape[0], down_ref.shape[1]
    rank = out_ref.shape[1]
    adapters = down_ref.shape[0] // rank
    every = lax.dot_general(
        down_ref[...],
        owned_ref[:, :columns],
        (((1,), (1,)), ((), ())),
        preferred_element_type=jnp.float32,
    )
    ids = owned_ref[:, columns:].astype(jnp.float32)
    ids_ref[...] = ids
    adapter = lax.broadcasted_iota(jnp.int32, (adapters, rank, rows), 0).astype(jnp.float32)
    chosen = adapter == jnp.transpose(ids)[:1].reshape(1, 1, rows)
    part = jnp.sum(jnp.where(chosen, every.reshape(adapters, rank, rows), 0.0), axis=0)
    for share in range(out_ref.shape[0]):
        out_ref[share] = part


def shrink_down(owned, down, up, shares, rank):
    rows = owned.shape[0]
    lanes = owned.shape[1] - down.shape[1]
    resident = pl.BlockSpec(memory_space=pltpu.VMEM)
    return pl.pallas_call(
        down_kernel,
        in_specs=[resident] * 3,
        out_specs=[resident] * 2,
        out_shape=[
            jax.ShapeDtypeStruct((shares, rank, rows), jnp.float32),
            jax.ShapeDtypeStruct((rows, lanes), jnp.float32),
        ],
        compiler_params=pltpu.CompilerParams(vmem_limit_bytes=16 * 1024 * 1024),
        cost_estimate=pl.CostEstimate(
            flops=2 * rows * down.size, bytes_accessed=4 * down.size, transcendentals=0
        ),
        name="shrink_down",
    )(owned, down, up)


def up_kernel(partials_ref, ids_ref, up_ref, out_ref):
    shares, rank, rows = partials_ref.shape
    maps = up_ref.shape[0]
    lanes = ids_ref.shape[1]
    shrink = partials_ref[0]
    for share in range(1, shares):
        shrink += partials_ref[share]
    fold = lax.broadcasted_iota(jnp.int32, (rank, maps), 1) % rank
    fold = (fold == lax.broadcasted_iota(jnp.int32, (rank, maps), 0)).astype(jnp.bfloat16)
    spread = lax.dot_general(
        shrink.astype(jnp.bfloat16),
        fold,
        (((0,), (0,)), ((), ())),
        preferred_element_type=jnp.float32,
    )
    ids = jnp.concatenate([ids_ref[...]] * (maps // lanes), axis=1)
    adapter = (lax.broadcasted_iota(jnp.int32, (1, maps), 1) // rank).astype(jnp.float32)
    out_ref[...] = jnp.dot(
        jnp.where(adapter == ids, spread, 0.0).astype(jnp.bfloat16),
        up_ref[...],
        preferred_element_type=jnp.float32,
    ).astype(jnp.bfloat16)


def expand_up(partials, ids, up):
    rows = partials.shape[2]
    resident = pl.BlockSpec(memory_space=pltpu.VMEM)
    return pl.pallas_call(
        up_kernel,
        in_specs=[resident] * 3,
        out_specs=resident,
        out_shape=jax.ShapeDtypeStruct((rows, up.shape[1]), jnp.bfloat16),
        compiler_params=pltpu.CompilerParams(vmem_limit_bytes=16 * 1024 * 1024),
        cost_estimate=pl.CostEstimate(
            flops=FAR_FLOPS, bytes_accessed=4 * up.size, transcendentals=0
        ),
        name="expand_up",
    )(partials, ids, up)


def finish_kernel(slots_ref, returned_ref, base_ref, *refs):
    across_refs, out_ref = refs[:-1], refs[-1]
    rows = returned_ref.shape[0]
    slot = lax.broadcasted_iota(jnp.int32, (rows, rows), 0)
    to_slots = (slot == slots_ref[...]).astype(jnp.bfloat16)
    delta = lax.dot_general(
        to_slots, returned_ref[...], (((0,), (0,)), ((), ())), preferred_element_type=jnp.float32
    )
    total = base_ref[...] + delta
    for across_ref in across_refs:
        total += across_ref[...].astype(jnp.float32)
    out_ref[...] = total.reshape(out_ref.shape).astype(out_ref.dtype)


def finish(row_slots, returned, base, across, out_shape):
    resident = pl.BlockSpec(memory_space=pltpu.VMEM)
    return pl.pallas_call(
        finish_kernel,
        in_specs=[resident] * (3 + len(across)),
        out_specs=resident,
        out_shape=jax.ShapeDtypeStruct(out_shape, jnp.bfloat16),
        compiler_params=pltpu.CompilerParams(vmem_limit_bytes=16 * 1024 * 1024),
        cost_estimate=pl.CostEstimate(
            flops=2 * returned.size * returned.shape[0],
            bytes_accessed=8 * returned.size,
            transcendentals=0,
        ),
        name="finish",
    )(row_slots, returned, base, *across)


def move(value, owners, target):
    pairs = []
    for d in range(owners):
        for pair in range(SIDE):
            for line in range(SIDE):
                to_pair, to_line = target(pair, line)
                if d % 2 == 0:
                    here, there = pair * SIDE + line, to_pair * SIDE + to_line
                else:
                    here, there = line * SIDE + pair, to_line * SIDE + to_pair
                pairs.append((d * SIDE * SIDE + here, d * SIDE * SIDE + there))
    return lax.ppermute(value, ("dp", "tensor"), pairs)


def after(value, *earlier):
    return lax.optimization_barrier((value,) + earlier)[0]


def on_device(
    queries,
    cached_key_rows,
    cached_value_rows,
    cache_fill_length,
    request_adapters,
    wo,
    adapter_down_weight,
    adapter_up_weight,
):
    owners = lax.axis_size("dp")
    shares = lax.axis_size("tensor")
    group_size = request_adapters.shape[0]
    owner_partial, rank, width = adapter_down_weight.shape
    capacity = group_size // owners
    steps = queries.shape[1]
    rows = group_size * steps

    owner_ids = request_adapters // owner_partial
    local_ids = request_adapters % owner_partial
    order = jnp.arange(group_size, dtype=jnp.int32)
    earlier = (owner_ids[:, None] == owner_ids[None, :]) & (order[:, None] > order[None, :])
    slots = owner_ids * capacity + jnp.sum(earlier.astype(jnp.int32), axis=1)
    row_slots = (slots[:, None] * steps + jnp.arange(steps, dtype=jnp.int32)).reshape(1, rows)
    row_locals = jnp.repeat(local_ids, steps)[None, :]

    attended = attend(queries, cached_key_rows, cached_value_rows, cache_fill_length)
    head_rows = lax.all_to_all(attended, "tensor", 0, 0, tiled=True).reshape(rows, width)

    payload = make_payload(head_rows, row_slots, row_locals)
    own, *others = project(after(head_rows, payload), wo)
    arrived = [
        move(part, owners, lambda pair, line, s=s: (pair, (line + s) % SIDE))
        for s, part in enumerate(others, start=1)
    ]
    owned = lax.all_to_all(
        payload.reshape(owners, capacity * steps, width + 128), "dp", 0, 0, tiled=True
    ).reshape(rows, width + 128)
    down = adapter_down_weight.reshape(owner_partial * rank, width)
    up = adapter_up_weight.reshape(owner_partial * rank, width)
    partial_shrink, ids = shrink_down(after(owned, own), down, up, shares, rank)
    partials = lax.all_to_all(partial_shrink, "tensor", 0, 0, tiled=True)
    delta = expand_up(after(partials, arrived[0], arrived[2]), ids, up)
    returned = lax.all_to_all(
        delta.reshape(owners, capacity * steps, width), "dp", 0, 0, tiled=True
    ).reshape(rows, width)

    along_line = [
        own[u] + sum(part[u].astype(jnp.float32) for part in arrived) for u in range(SIDE)
    ]
    across = [
        move(
            along_line[u].astype(jnp.bfloat16),
            owners,
            lambda pair, line, u=u: ((pair + u) % SIDE, line),
        )
        for u in range(1, SIDE)
    ]
    return finish(
        row_slots, returned, along_line[0], across, (group_size, steps, width)
    )


def solution(mesh):
    in_specs = (
        P(("dp", "tensor"), None, None, None),
        P(("dp", "tensor"), None, None, None),
        P(("dp", "tensor"), None, None, None),
        P(("dp", "tensor")),
        P("dp"),
        P("tensor", None),
        P("dp", None, "tensor"),
        P("dp", None, "tensor"),
    )
    out_specs = P("dp", None, "tensor")
    return jax.shard_map(
        on_device, mesh=mesh, in_specs=in_specs, out_specs=out_specs, check_vma=False
    )
```

```python
import math

import jax
import jax.numpy as jnp
from jax import lax
from jax.experimental import pallas as pl
from jax.experimental.pallas import tpu as pltpu
from jax.sharding import PartitionSpec as P

NEG_FILL = -1e30
FAR_FLOPS = 20_000_000_000
SIDE = 4


def torus_place():
    tensor = lax.axis_index("tensor")
    y, x = tensor // SIDE, lax.rem(tensor, SIDE)
    odd = lax.rem(lax.axis_index("dp"), 2)
    pair, line = y + odd * (x - y), x + odd * (y - x)
    pair_stride = SIDE + odd * (1 - SIDE)
    return pair, line, pair_stride, SIDE + 1 - pair_stride


def attend_kernel(
    fill_ref, queries_ref, keys_ref, values_ref, out_ref,
    query_buf, key_buf, value_buf, score_buf, weight_buf, grouped_buf,
    query_sem, key_sem, value_sem,
):
    requests, steps, heads, head_dim = query_buf.shape
    kv_heads, cache_len = key_buf.shape[1], key_buf.shape[2]
    per_group = heads // kv_heads
    group_rows = steps * per_group
    query_copy = pltpu.make_async_copy(queries_ref, query_buf, query_sem)
    key_copies = [
        pltpu.make_async_copy(keys_ref.at[r], key_buf.at[r], key_sem.at[r]) for r in range(requests)
    ]
    value_copies = [
        pltpu.make_async_copy(values_ref.at[r], value_buf.at[r], value_sem.at[r])
        for r in range(requests)
    ]
    query_copy.start()
    for copy in key_copies:
        copy.start()
    position = lax.broadcasted_iota(jnp.int32, (group_rows, cache_len), 1)
    step_of = lax.broadcasted_iota(jnp.int32, (group_rows, cache_len), 0) // per_group
    reach = position + steps - step_of
    query_copy.wait()
    for r in range(requests):
        every = query_buf[r].astype(jnp.float32)
        key_copies[r].wait()
        value_copies[r].start()
        for k in range(kv_heads):
            grouped = every[:, k * per_group : (k + 1) * per_group, :]
            grouped = grouped.reshape(group_rows, head_dim).astype(jnp.bfloat16)
            score_buf[r * kv_heads + k] = lax.dot_general(
                grouped,
                key_buf[r, k],
                (((1,), (1,)), ((), ())),
                preferred_element_type=jnp.float32,
            )
    for r in range(requests):
        valid = reach <= fill_ref[r]
        for k in range(kv_heads):
            scores = score_buf[r * kv_heads + k] * (1.0 / math.sqrt(head_dim))
            scores = jnp.where(valid, scores, NEG_FILL)
            raised = jnp.exp(scores - jnp.max(scores, axis=1, keepdims=True))
            weights = raised * (1.0 / jnp.sum(raised, axis=1, keepdims=True))
            weight_buf[r * kv_heads + k] = weights.astype(jnp.bfloat16)
    for r in range(requests):
        value_copies[r].wait()
        for k in range(kv_heads):
            grouped_buf[k, r * group_rows : (r + 1) * group_rows] = jnp.dot(
                weight_buf[r * kv_heads + k], value_buf[r, k], preferred_element_type=jnp.float32
            ).astype(jnp.bfloat16)
    every_rows = requests * group_rows
    rows = requests * steps
    old = lax.broadcasted_iota(jnp.int32, (every_rows, every_rows), 1)
    new = lax.broadcasted_iota(jnp.int32, (every_rows, every_rows), 0)
    turn = (old == new % rows * per_group + new // rows).astype(jnp.bfloat16)
    for k in range(kv_heads):
        turned = jnp.dot(turn, grouped_buf[k], preferred_element_type=jnp.float32)
        turned = turned.astype(jnp.bfloat16)
        for g in range(per_group):
            block, at = k * (per_group // 2) + g // 2, g % 2 * head_dim
            piece = turned[g * rows : (g + 1) * rows]
            out_ref[block, :, at : at + head_dim] = piece


def attend(queries, cached_key_rows, cached_value_rows, cache_fill_length):
    requests, steps, heads, head_dim = queries.shape
    kv_heads, cache_len = cached_key_rows.shape[1:3]
    blocks, rows = heads // 2, requests * steps
    pairs, group_rows = requests * kv_heads, steps * heads // kv_heads
    distant = pl.BlockSpec(memory_space=pl.ANY)
    return pl.pallas_call(
        attend_kernel,
        in_specs=[pl.BlockSpec(memory_space=pltpu.SMEM)] + [distant] * 3,
        out_specs=pl.BlockSpec(memory_space=pltpu.VMEM),
        out_shape=jax.ShapeDtypeStruct((blocks, rows, 2 * head_dim), jnp.bfloat16),
        scratch_shapes=[
            pltpu.VMEM(queries.shape, jnp.bfloat16),
            pltpu.VMEM(cached_key_rows.shape, jnp.bfloat16),
            pltpu.VMEM(cached_value_rows.shape, jnp.bfloat16),
            pltpu.VMEM((pairs, group_rows, cache_len), jnp.float32),
            pltpu.VMEM((pairs, group_rows, cache_len), jnp.bfloat16),
            pltpu.VMEM((kv_heads, requests * group_rows, head_dim), jnp.bfloat16),
            pltpu.SemaphoreType.DMA,
            pltpu.SemaphoreType.DMA((requests,)),
            pltpu.SemaphoreType.DMA((requests,)),
        ],
        compiler_params=pltpu.CompilerParams(vmem_limit_bytes=60 * 1024 * 1024),
        cost_estimate=pl.CostEstimate(
            flops=4 * rows * heads * cache_len * head_dim,
            bytes_accessed=2 * 2 * cached_key_rows.size,
            transcendentals=rows * heads * cache_len,
        ),
        name="attend",
    )(cache_fill_length, queries, cached_key_rows, cached_value_rows)


def slot_kernel(slots_ref, locals_ref, hit_ref, ids_ref):
    rows, lanes = ids_ref.shape
    slot = lax.broadcasted_iota(jnp.int32, (rows, rows), 0)
    hit = (slot == slots_ref[...]).astype(jnp.bfloat16)
    hit_ref[...] = hit
    ids = locals_ref[...].astype(jnp.float32).astype(jnp.bfloat16)
    ids_ref[...] = lax.dot_general(
        hit,
        jnp.broadcast_to(ids, (lanes, rows)),
        (((1,), (1,)), ((), ())),
        preferred_element_type=jnp.float32,
    ).astype(jnp.bfloat16)


def slot_map(row_slots, row_locals):
    rows = row_slots.shape[1]
    resident = pl.BlockSpec(memory_space=pltpu.VMEM)
    return pl.pallas_call(
        slot_kernel,
        in_specs=[resident] * 2,
        out_specs=[resident] * 2,
        out_shape=[
            jax.ShapeDtypeStruct((rows, rows), jnp.bfloat16),
            jax.ShapeDtypeStruct((rows, 128), jnp.bfloat16),
        ],
        compiler_params=pltpu.CompilerParams(vmem_limit_bytes=16 * 1024 * 1024),
        cost_estimate=pl.CostEstimate(
            flops=2 * rows * rows * 128, bytes_accessed=4 * rows * rows, transcendentals=0
        ),
        name="slot_map",
    )(row_slots, row_locals)


def payload_kernel(rows_ref, hit_ref, ids_ref, out_ref):
    width = rows_ref.shape[1]
    out_ref[:, :width] = jnp.dot(
        hit_ref[...], rows_ref[...], preferred_element_type=jnp.float32
    ).astype(jnp.bfloat16)
    out_ref[:, width:] = ids_ref[...]


def make_payload(head_rows, hit, ids):
    rows, width = head_rows.shape
    resident = pl.BlockSpec(memory_space=pltpu.VMEM)
    return pl.pallas_call(
        payload_kernel,
        in_specs=[resident] * 3,
        out_specs=resident,
        out_shape=jax.ShapeDtypeStruct((rows, width + ids.shape[1]), jnp.bfloat16),
        compiler_params=pltpu.CompilerParams(vmem_limit_bytes=16 * 1024 * 1024),
        cost_estimate=pl.CostEstimate(
            flops=2 * rows * rows * width, bytes_accessed=8 * rows * width, transcendentals=0
        ),
        name="make_payload",
    )(head_rows, hit, ids)


def project_kernel(rows_ref, wo_ref, *refs):
    own_ref, own_buf, own_sem = refs[0], refs[SIDE], refs[SIDE + 1]
    out_refs = (own_buf,) + refs[1:SIDE]
    pair, line, pair_stride, line_stride = torus_place()
    width = rows_ref.shape[1]
    for s, out_ref in enumerate(out_refs):
        along = lax.rem(line + s, SIDE)
        for u in range(SIDE):
            across = lax.rem(pair + u, SIDE)
            at = pl.multiple_of((across * pair_stride + along * line_stride) * width, width)
            part = jnp.dot(
                rows_ref[...], wo_ref[:, pl.ds(at, width)], preferred_element_type=jnp.float32
            )
            out_ref[u] = part.astype(out_ref.dtype)
        if s == 0:
            own_copy = pltpu.make_async_copy(own_buf, own_ref, own_sem)
            own_copy.start()
    own_copy.wait()


def project(head_rows, wo):
    rows, depth = head_rows.shape
    width = wo.shape[1] // (SIDE * SIDE)
    resident = pl.BlockSpec(memory_space=pltpu.VMEM)
    return pl.pallas_call(
        project_kernel,
        in_specs=[resident] * 2,
        out_specs=[pl.BlockSpec(memory_space=pltpu.HBM)] + [resident] * (SIDE - 1),
        out_shape=[pltpu.HBM((SIDE, rows, width), jnp.float32)]
        + [jax.ShapeDtypeStruct((SIDE, rows, width), jnp.bfloat16)] * (SIDE - 1),
        scratch_shapes=[pltpu.VMEM((SIDE, rows, width), jnp.float32), pltpu.SemaphoreType.DMA],
        compiler_params=pltpu.CompilerParams(vmem_limit_bytes=16 * 1024 * 1024),
        cost_estimate=pl.CostEstimate(
            flops=2 * rows * depth * wo.shape[1],
            bytes_accessed=2 * wo.size + 3 * rows * wo.shape[1],
            transcendentals=0,
        ),
        name="project",
    )(head_rows, wo)


def down_kernel(owned_ref, down_ref, up_ref, out_ref, ids_ref):
    del up_ref
    rows, columns = owned_ref.shape[0], down_ref.shape[1]
    rank = out_ref.shape[1]
    adapters = down_ref.shape[0] // rank
    every = lax.dot_general(
        down_ref[...],
        owned_ref[:, :columns],
        (((1,), (1,)), ((), ())),
        preferred_element_type=jnp.float32,
    )
    ids = owned_ref[:, columns:].astype(jnp.float32)
    ids_ref[...] = ids
    adapter = lax.broadcasted_iota(jnp.int32, (adapters, rank, rows), 0).astype(jnp.float32)
    chosen = adapter == jnp.transpose(ids)[:1].reshape(1, 1, rows)
    part = jnp.sum(jnp.where(chosen, every.reshape(adapters, rank, rows), 0.0), axis=0)
    for share in range(out_ref.shape[0]):
        out_ref[share] = part.astype(out_ref.dtype)


def shrink_down(owned, down, up, shares, rank):
    rows = owned.shape[0]
    lanes = owned.shape[1] - down.shape[1]
    resident = pl.BlockSpec(memory_space=pltpu.VMEM)
    return pl.pallas_call(
        down_kernel,
        in_specs=[resident] * 3,
        out_specs=[resident] * 2,
        out_shape=[
            jax.ShapeDtypeStruct((shares, rank, rows), jnp.bfloat16),
            jax.ShapeDtypeStruct((rows, lanes), jnp.float32),
        ],
        compiler_params=pltpu.CompilerParams(vmem_limit_bytes=16 * 1024 * 1024),
        cost_estimate=pl.CostEstimate(
            flops=2 * rows * down.size, bytes_accessed=4 * down.size, transcendentals=0
        ),
        name="shrink_down",
    )(owned, down, up)


def up_kernel(partials_ref, ids_ref, up_ref, out_ref):
    shares, rank, rows = partials_ref.shape
    maps = up_ref.shape[0]
    lanes = ids_ref.shape[1]
    shrink = partials_ref[0].astype(jnp.float32)
    for share in range(1, shares):
        shrink += partials_ref[share].astype(jnp.float32)
    fold = lax.broadcasted_iota(jnp.int32, (rank, maps), 1) % rank
    fold = (fold == lax.broadcasted_iota(jnp.int32, (rank, maps), 0)).astype(jnp.bfloat16)
    spread = lax.dot_general(
        shrink.astype(jnp.bfloat16),
        fold,
        (((0,), (0,)), ((), ())),
        preferred_element_type=jnp.float32,
    )
    ids = jnp.concatenate([ids_ref[...]] * (maps // lanes), axis=1)
    adapter = (lax.broadcasted_iota(jnp.int32, (1, maps), 1) // rank).astype(jnp.float32)
    out_ref[...] = jnp.dot(
        jnp.where(adapter == ids, spread, 0.0).astype(jnp.bfloat16),
        up_ref[...],
        preferred_element_type=jnp.float32,
    ).astype(jnp.bfloat16)


def expand_up(partials, ids, up):
    rows = partials.shape[2]
    resident = pl.BlockSpec(memory_space=pltpu.VMEM)
    return pl.pallas_call(
        up_kernel,
        in_specs=[resident] * 3,
        out_specs=resident,
        out_shape=jax.ShapeDtypeStruct((rows, up.shape[1]), jnp.bfloat16),
        compiler_params=pltpu.CompilerParams(vmem_limit_bytes=16 * 1024 * 1024),
        cost_estimate=pl.CostEstimate(
            flops=FAR_FLOPS, bytes_accessed=4 * up.size, transcendentals=0
        ),
        name="expand_up",
    )(partials, ids, up)


def finish_kernel(hit_ref, returned_ref, base_ref, *refs):
    across_refs, out_ref = refs[:-1], refs[-1]
    delta = lax.dot_general(
        hit_ref[...], returned_ref[...], (((0,), (0,)), ((), ())), preferred_element_type=jnp.float32
    )
    total = base_ref[...] + delta
    for across_ref in across_refs:
        total += across_ref[...].astype(jnp.float32)
    out_ref[...] = total.reshape(out_ref.shape).astype(out_ref.dtype)


def finish(hit, returned, base, across, out_shape):
    resident = pl.BlockSpec(memory_space=pltpu.VMEM)
    return pl.pallas_call(
        finish_kernel,
        in_specs=[resident] * (3 + len(across)),
        out_specs=resident,
        out_shape=jax.ShapeDtypeStruct(out_shape, jnp.bfloat16),
        compiler_params=pltpu.CompilerParams(vmem_limit_bytes=16 * 1024 * 1024),
        cost_estimate=pl.CostEstimate(
            flops=2 * returned.size * returned.shape[0],
            bytes_accessed=8 * returned.size,
            transcendentals=0,
        ),
        name="finish",
    )(hit, returned, base, *across)


def move(value, owners, target):
    pairs = []
    for d in range(owners):
        for pair in range(SIDE):
            for line in range(SIDE):
                to_pair, to_line = target(pair, line)
                if d % 2 == 0:
                    here, there = pair * SIDE + line, to_pair * SIDE + to_line
                else:
                    here, there = line * SIDE + pair, to_line * SIDE + to_pair
                pairs.append((d * SIDE * SIDE + here, d * SIDE * SIDE + there))
    return lax.ppermute(value, ("dp", "tensor"), pairs)


def after(value, *earlier):
    return lax.optimization_barrier((value,) + earlier)[0]


def on_device(
    queries,
    cached_key_rows,
    cached_value_rows,
    cache_fill_length,
    request_adapters,
    wo,
    adapter_down_weight,
    adapter_up_weight,
):
    owners = lax.axis_size("dp")
    shares = lax.axis_size("tensor")
    group_size = request_adapters.shape[0]
    owner_partial, rank, width = adapter_down_weight.shape
    capacity = group_size // owners
    steps = queries.shape[1]
    rows = group_size * steps

    owner_ids = request_adapters // owner_partial
    local_ids = request_adapters % owner_partial
    order = jnp.arange(group_size, dtype=jnp.int32)
    earlier = (owner_ids[:, None] == owner_ids[None, :]) & (order[:, None] > order[None, :])
    slots = owner_ids * capacity + jnp.sum(earlier.astype(jnp.int32), axis=1)
    row_slots = (slots[:, None] * steps + jnp.arange(steps, dtype=jnp.int32)).reshape(1, rows)
    row_locals = jnp.repeat(local_ids, steps)[None, :]
    hit, id_lanes = slot_map(row_slots, row_locals)

    attended = attend(queries, cached_key_rows, cached_value_rows, cache_fill_length)
    head_rows = lax.all_to_all(attended, "tensor", 0, 0, tiled=True).reshape(rows, width)

    payload = make_payload(head_rows, hit, id_lanes)
    own, *others = project(after(head_rows, payload), wo)
    arrived = [
        move(part, owners, lambda pair, line, s=s: (pair, (line + s) % SIDE))
        for s, part in enumerate(others, start=1)
    ]
    owned = lax.all_to_all(
        payload.reshape(owners, capacity * steps, width + 128), "dp", 0, 0, tiled=True
    ).reshape(rows, width + 128)
    down = adapter_down_weight.reshape(owner_partial * rank, width)
    up = adapter_up_weight.reshape(owner_partial * rank, width)
    partial_shrink, ids = shrink_down(after(owned, own), down, up, shares, rank)
    partials = lax.all_to_all(partial_shrink, "tensor", 0, 0, tiled=True)
    delta = expand_up(after(partials, arrived[0], arrived[2]), ids, up)
    returned = lax.all_to_all(
        delta.reshape(owners, capacity * steps, width), "dp", 0, 0, tiled=True
    ).reshape(rows, width)

    along_line = [
        own[u] + sum(part[u].astype(jnp.float32) for part in arrived) for u in range(SIDE)
    ]
    across = [
        move(
            along_line[u].astype(jnp.bfloat16),
            owners,
            lambda pair, line, u=u: ((pair + u) % SIDE, line),
        )
        for u in range(1, SIDE)
    ]
    return finish(
        hit, returned, along_line[0], across, (group_size, steps, width)
    )


def solution(mesh):
    in_specs = (
        P(("dp", "tensor"), None, None, None),
        P(("dp", "tensor"), None, None, None),
        P(("dp", "tensor"), None, None, None),
        P(("dp", "tensor")),
        P("dp"),
        P("tensor", None),
        P("dp", None, "tensor"),
        P("dp", None, "tensor"),
    )
    out_specs = P("dp", None, "tensor")
    return jax.shard_map(
        on_device, mesh=mesh, in_specs=in_specs, out_specs=out_specs, check_vma=False
    )
```

```python
import math

import jax
import jax.numpy as jnp
from jax import lax
from jax.experimental import pallas as pl
from jax.experimental.pallas import tpu as pltpu
from jax.sharding import PartitionSpec as P

NEG_FILL = -1e30
FAR_FLOPS = 20_000_000_000
SIDE = 4


def torus_place():
    tensor = lax.axis_index("tensor")
    y, x = tensor // SIDE, lax.rem(tensor, SIDE)
    odd = lax.rem(lax.axis_index("dp"), 2)
    pair, line = y + odd * (x - y), x + odd * (y - x)
    pair_stride = SIDE + odd * (1 - SIDE)
    return pair, line, pair_stride, SIDE + 1 - pair_stride


def attend_kernel(
    fill_ref, queries_ref, keys_ref, values_ref, out_ref,
    query_buf, key_buf, value_buf, score_buf, weight_buf, grouped_buf,
    query_sem, key_sem, value_sem,
):
    requests, steps, heads, head_dim = query_buf.shape
    kv_heads, cache_len = key_buf.shape[1], key_buf.shape[2]
    per_group = heads // kv_heads
    group_rows = steps * per_group
    query_copy = pltpu.make_async_copy(queries_ref, query_buf, query_sem)
    key_copies = [
        pltpu.make_async_copy(keys_ref.at[r], key_buf.at[r], key_sem.at[r]) for r in range(requests)
    ]
    value_copies = [
        pltpu.make_async_copy(values_ref.at[r], value_buf.at[r], value_sem.at[r])
        for r in range(requests)
    ]
    query_copy.start()
    for copy in key_copies:
        copy.start()
    position = lax.broadcasted_iota(jnp.int32, (group_rows, cache_len), 1)
    step_of = lax.broadcasted_iota(jnp.int32, (group_rows, cache_len), 0) // per_group
    reach = position + steps - step_of
    query_copy.wait()
    for r in range(requests):
        every = query_buf[r].astype(jnp.float32)
        key_copies[r].wait()
        value_copies[r].start()
        for k in range(kv_heads):
            grouped = every[:, k * per_group : (k + 1) * per_group, :]
            grouped = grouped.reshape(group_rows, head_dim).astype(jnp.bfloat16)
            score_buf[r * kv_heads + k] = lax.dot_general(
                grouped,
                key_buf[r, k],
                (((1,), (1,)), ((), ())),
                preferred_element_type=jnp.float32,
            )
    for r in range(requests):
        valid = reach <= fill_ref[r]
        for k in range(kv_heads):
            scores = score_buf[r * kv_heads + k] * (1.0 / math.sqrt(head_dim))
            scores = jnp.where(valid, scores, NEG_FILL)
            raised = jnp.exp(scores - jnp.max(scores, axis=1, keepdims=True))
            weights = raised * (1.0 / jnp.sum(raised, axis=1, keepdims=True))
            weight_buf[r * kv_heads + k] = weights.astype(jnp.bfloat16)
    for r in range(requests):
        value_copies[r].wait()
        for k in range(kv_heads):
            grouped_buf[k, r * group_rows : (r + 1) * group_rows] = jnp.dot(
                weight_buf[r * kv_heads + k], value_buf[r, k], preferred_element_type=jnp.float32
            ).astype(jnp.bfloat16)
    every_rows = requests * group_rows
    rows = requests * steps
    old = lax.broadcasted_iota(jnp.int32, (every_rows, every_rows), 1)
    new = lax.broadcasted_iota(jnp.int32, (every_rows, every_rows), 0)
    turn = (old == new % rows * per_group + new // rows).astype(jnp.bfloat16)
    for k in range(kv_heads):
        turned = jnp.dot(turn, grouped_buf[k], preferred_element_type=jnp.float32)
        turned = turned.astype(jnp.bfloat16)
        for g in range(per_group):
            block, at = k * (per_group // 2) + g // 2, g % 2 * head_dim
            piece = turned[g * rows : (g + 1) * rows]
            out_ref[block, :, at : at + head_dim] = piece


def attend(queries, cached_key_rows, cached_value_rows, cache_fill_length):
    requests, steps, heads, head_dim = queries.shape
    kv_heads, cache_len = cached_key_rows.shape[1:3]
    blocks, rows = heads // 2, requests * steps
    pairs, group_rows = requests * kv_heads, steps * heads // kv_heads
    distant = pl.BlockSpec(memory_space=pl.ANY)
    return pl.pallas_call(
        attend_kernel,
        in_specs=[pl.BlockSpec(memory_space=pltpu.SMEM)] + [distant] * 3,
        out_specs=pl.BlockSpec(memory_space=pltpu.VMEM),
        out_shape=jax.ShapeDtypeStruct((blocks, rows, 2 * head_dim), jnp.bfloat16),
        scratch_shapes=[
            pltpu.VMEM(queries.shape, jnp.bfloat16),
            pltpu.VMEM(cached_key_rows.shape, jnp.bfloat16),
            pltpu.VMEM(cached_value_rows.shape, jnp.bfloat16),
            pltpu.VMEM((pairs, group_rows, cache_len), jnp.float32),
            pltpu.VMEM((pairs, group_rows, cache_len), jnp.bfloat16),
            pltpu.VMEM((kv_heads, requests * group_rows, head_dim), jnp.bfloat16),
            pltpu.SemaphoreType.DMA,
            pltpu.SemaphoreType.DMA((requests,)),
            pltpu.SemaphoreType.DMA((requests,)),
        ],
        compiler_params=pltpu.CompilerParams(vmem_limit_bytes=60 * 1024 * 1024),
        cost_estimate=pl.CostEstimate(
            flops=4 * rows * heads * cache_len * head_dim,
            bytes_accessed=2 * 2 * cached_key_rows.size,
            transcendentals=rows * heads * cache_len,
        ),
        name="attend",
    )(cache_fill_length, queries, cached_key_rows, cached_value_rows)


def slot_kernel(slots_ref, locals_ref, hit_ref, ids_ref):
    owners, capacity, lanes = ids_ref.shape
    rows = hit_ref.shape[0]
    slot = lax.broadcasted_iota(jnp.int32, (rows, rows), 0)
    hit_ref[...] = (slot == slots_ref[...]).astype(jnp.bfloat16)
    steps = rows // owners // capacity
    wanted = lax.broadcasted_iota(jnp.int32, (owners * capacity, 1), 0) * steps
    pick = (wanted == slots_ref[...]).astype(jnp.bfloat16)
    ids = locals_ref[...].astype(jnp.float32).astype(jnp.bfloat16)
    spread = lax.dot_general(
        pick,
        jnp.broadcast_to(ids, (lanes, rows)),
        (((1,), (1,)), ((), ())),
        preferred_element_type=jnp.float32,
    )
    ids_ref[...] = spread.reshape(owners, capacity, lanes).astype(jnp.bfloat16)


def slot_map(row_slots, row_locals, owners, capacity):
    rows = row_slots.shape[1]
    resident = pl.BlockSpec(memory_space=pltpu.VMEM)
    return pl.pallas_call(
        slot_kernel,
        in_specs=[resident] * 2,
        out_specs=[resident] * 2,
        out_shape=[
            jax.ShapeDtypeStruct((rows, rows), jnp.bfloat16),
            jax.ShapeDtypeStruct((owners, capacity, 128), jnp.bfloat16),
        ],
        compiler_params=pltpu.CompilerParams(vmem_limit_bytes=16 * 1024 * 1024),
        cost_estimate=pl.CostEstimate(
            flops=2 * rows * rows * 128, bytes_accessed=4 * rows * rows, transcendentals=0
        ),
        name="slot_map",
    )(row_slots, row_locals)


def payload_kernel(rows_ref, hit_ref, ids_ref, out_ref):
    owners, tiles, tile_rows, lanes = out_ref.shape
    run = (tiles - 1) // 2
    part = jnp.dot(hit_ref[...], rows_ref[...], preferred_element_type=jnp.float32)
    for half in range(2):
        piece = part[:, half * lanes : (half + 1) * lanes].reshape(owners, run, tile_rows, lanes)
        out_ref[:, half * run : (half + 1) * run] = piece.astype(jnp.bfloat16)
    out_ref[:, tiles - 1] = ids_ref[...]


def make_payload(head_rows, hit, ids):
    rows, width = head_rows.shape
    owners, tile_rows, lanes = ids.shape
    tiles = rows // owners // tile_rows * (width // lanes) + 1
    resident = pl.BlockSpec(memory_space=pltpu.VMEM)
    return pl.pallas_call(
        payload_kernel,
        in_specs=[resident] * 3,
        out_specs=resident,
        out_shape=jax.ShapeDtypeStruct((owners, tiles, tile_rows, lanes), jnp.bfloat16),
        compiler_params=pltpu.CompilerParams(vmem_limit_bytes=16 * 1024 * 1024),
        cost_estimate=pl.CostEstimate(
            flops=2 * rows * rows * width, bytes_accessed=8 * rows * width, transcendentals=0
        ),
        name="make_payload",
    )(head_rows, hit, ids)


def project_kernel(rows_ref, wo_ref, own_ref, far_ref, near_1_ref, near_3_ref, *scratch):
    own_buf, far_buf, sems = scratch
    pair, line, pair_stride, line_stride = torus_place()
    width = rows_ref.shape[1]
    copies = []
    for s, part_ref in ((0, own_buf), (2, far_buf), (1, near_1_ref), (3, near_3_ref)):
        along = lax.rem(line + s, SIDE)
        for u in range(SIDE):
            across = lax.rem(pair + u, SIDE)
            at = pl.multiple_of((across * pair_stride + along * line_stride) * width, width)
            part = jnp.dot(
                rows_ref[...], wo_ref[:, pl.ds(at, width)], preferred_element_type=jnp.float32
            )
            part_ref[u] = part.astype(part_ref.dtype)
        if s % 2 == 0:
            target = own_ref if s == 0 else far_ref
            copies.append(pltpu.make_async_copy(part_ref, target, sems.at[s // 2]))
            copies[-1].start()
    for copy in copies:
        copy.wait()


def project(head_rows, wo):
    rows, depth = head_rows.shape
    width = wo.shape[1] // (SIDE * SIDE)
    shape = (SIDE, rows, width)
    resident = pl.BlockSpec(memory_space=pltpu.VMEM)
    distant = pl.BlockSpec(memory_space=pltpu.HBM)
    own, far, near_1, near_3 = pl.pallas_call(
        project_kernel,
        in_specs=[resident] * 2,
        out_specs=[distant] * 2 + [resident] * 2,
        out_shape=[pltpu.HBM(shape, jnp.float32), pltpu.HBM(shape, jnp.bfloat16)]
        + [jax.ShapeDtypeStruct(shape, jnp.bfloat16)] * 2,
        scratch_shapes=[
            pltpu.VMEM(shape, jnp.float32),
            pltpu.VMEM(shape, jnp.bfloat16),
            pltpu.SemaphoreType.DMA((2,)),
        ],
        compiler_params=pltpu.CompilerParams(vmem_limit_bytes=16 * 1024 * 1024),
        cost_estimate=pl.CostEstimate(
            flops=2 * rows * depth * wo.shape[1],
            bytes_accessed=2 * wo.size + 3 * rows * wo.shape[1],
            transcendentals=0,
        ),
        name="project",
    )(head_rows, wo)
    return own, near_1, far, near_3


def down_kernel(owned_ref, down_ref, up_ref, out_ref, ids_ref):
    del up_ref
    sources, tiles, capacity, lanes = owned_ref.shape
    run = (tiles - 1) // 2
    rank, rows = out_ref.shape[1:]
    adapters = down_ref.shape[0] // rank
    every = 0.0
    for half in range(2):
        piece = owned_ref[:, half * run : (half + 1) * run].astype(jnp.float32)
        every += lax.dot_general(
            down_ref[:, half * lanes : (half + 1) * lanes],
            piece.reshape(rows, lanes).astype(jnp.bfloat16),
            (((1,), (1,)), ((), ())),
            preferred_element_type=jnp.float32,
        )
    tile = owned_ref[:, tiles - 1].astype(jnp.float32)
    ids = jnp.concatenate(
        [
            jnp.broadcast_to(tile[:, k : k + 1], (sources, rows // sources // capacity, lanes))
            for k in range(capacity)
        ],
        axis=1,
    ).reshape(rows, lanes)
    ids_ref[...] = ids
    adapter = lax.broadcasted_iota(jnp.int32, (adapters, rank, rows), 0).astype(jnp.float32)
    chosen = adapter == jnp.transpose(ids)[:1].reshape(1, 1, rows)
    part = jnp.sum(jnp.where(chosen, every.reshape(adapters, rank, rows), 0.0), axis=0)
    for share in range(out_ref.shape[0]):
        out_ref[share] = part.astype(out_ref.dtype)


def shrink_down(owned, down, up, shares, rank):
    sources, tiles, tile_rows, lanes = owned.shape
    rows = sources * (tiles - 1) // 2 * tile_rows
    resident = pl.BlockSpec(memory_space=pltpu.VMEM)
    return pl.pallas_call(
        down_kernel,
        in_specs=[resident] * 3,
        out_specs=[resident] * 2,
        out_shape=[
            jax.ShapeDtypeStruct((shares, rank, rows), jnp.bfloat16),
            jax.ShapeDtypeStruct((rows, lanes), jnp.float32),
        ],
        compiler_params=pltpu.CompilerParams(vmem_limit_bytes=16 * 1024 * 1024),
        cost_estimate=pl.CostEstimate(
            flops=2 * rows * down.size, bytes_accessed=4 * down.size, transcendentals=0
        ),
        name="shrink_down",
    )(owned, down, up)


def up_kernel(partials_ref, ids_ref, up_ref, out_ref):
    shares, rank, rows = partials_ref.shape
    maps = up_ref.shape[0]
    lanes = ids_ref.shape[1]
    shrink = partials_ref[0].astype(jnp.float32)
    for share in range(1, shares):
        shrink += partials_ref[share].astype(jnp.float32)
    fold = lax.broadcasted_iota(jnp.int32, (rank, maps), 1) % rank
    fold = (fold == lax.broadcasted_iota(jnp.int32, (rank, maps), 0)).astype(jnp.bfloat16)
    spread = lax.dot_general(
        shrink.astype(jnp.bfloat16),
        fold,
        (((0,), (0,)), ((), ())),
        preferred_element_type=jnp.float32,
    )
    ids = jnp.concatenate([ids_ref[...]] * (maps // lanes), axis=1)
    adapter = (lax.broadcasted_iota(jnp.int32, (1, maps), 1) // rank).astype(jnp.float32)
    out_ref[...] = jnp.dot(
        jnp.where(adapter == ids, spread, 0.0).astype(jnp.bfloat16),
        up_ref[...],
        preferred_element_type=jnp.float32,
    ).astype(jnp.bfloat16)


def expand_up(partials, ids, up):
    rows = partials.shape[2]
    resident = pl.BlockSpec(memory_space=pltpu.VMEM)
    return pl.pallas_call(
        up_kernel,
        in_specs=[resident] * 3,
        out_specs=resident,
        out_shape=jax.ShapeDtypeStruct((rows, up.shape[1]), jnp.bfloat16),
        compiler_params=pltpu.CompilerParams(vmem_limit_bytes=16 * 1024 * 1024),
        cost_estimate=pl.CostEstimate(
            flops=FAR_FLOPS, bytes_accessed=4 * up.size, transcendentals=0
        ),
        name="expand_up",
    )(partials, ids, up)


def finish_kernel(hit_ref, returned_ref, base_ref, *refs):
    across_refs, out_ref = refs[:-1], refs[-1]
    delta = lax.dot_general(
        hit_ref[...], returned_ref[...], (((0,), (0,)), ((), ())), preferred_element_type=jnp.float32
    )
    total = base_ref[...] + delta
    for across_ref in across_refs:
        total += across_ref[...].astype(jnp.float32)
    out_ref[...] = total.reshape(out_ref.shape).astype(out_ref.dtype)


def finish(hit, returned, base, across, out_shape):
    resident = pl.BlockSpec(memory_space=pltpu.VMEM)
    return pl.pallas_call(
        finish_kernel,
        in_specs=[resident] * (3 + len(across)),
        out_specs=resident,
        out_shape=jax.ShapeDtypeStruct(out_shape, jnp.bfloat16),
        compiler_params=pltpu.CompilerParams(vmem_limit_bytes=16 * 1024 * 1024),
        cost_estimate=pl.CostEstimate(
            flops=2 * returned.size * returned.shape[0],
            bytes_accessed=8 * returned.size,
            transcendentals=0,
        ),
        name="finish",
    )(hit, returned, base, *across)


def move(value, owners, target):
    pairs = []
    for d in range(owners):
        for pair in range(SIDE):
            for line in range(SIDE):
                to_pair, to_line = target(pair, line)
                if d % 2 == 0:
                    here, there = pair * SIDE + line, to_pair * SIDE + to_line
                else:
                    here, there = line * SIDE + pair, to_line * SIDE + to_pair
                pairs.append((d * SIDE * SIDE + here, d * SIDE * SIDE + there))
    return lax.ppermute(value, ("dp", "tensor"), pairs)


def after(value, *earlier):
    return lax.optimization_barrier((value,) + earlier)[0]


def on_device(
    queries,
    cached_key_rows,
    cached_value_rows,
    cache_fill_length,
    request_adapters,
    wo,
    adapter_down_weight,
    adapter_up_weight,
):
    owners = lax.axis_size("dp")
    shares = lax.axis_size("tensor")
    group_size = request_adapters.shape[0]
    owner_partial, rank, width = adapter_down_weight.shape
    capacity = group_size // owners
    steps = queries.shape[1]
    rows = group_size * steps

    owner_ids = request_adapters // owner_partial
    local_ids = request_adapters % owner_partial
    order = jnp.arange(group_size, dtype=jnp.int32)
    earlier = (owner_ids[:, None] == owner_ids[None, :]) & (order[:, None] > order[None, :])
    slots = owner_ids * capacity + jnp.sum(earlier.astype(jnp.int32), axis=1)
    row_slots = (slots[:, None] * steps + jnp.arange(steps, dtype=jnp.int32)).reshape(1, rows)
    row_locals = jnp.repeat(local_ids, steps)[None, :]
    hit, id_lanes = slot_map(row_slots, row_locals, owners, capacity)

    attended = attend(queries, cached_key_rows, cached_value_rows, cache_fill_length)
    head_rows = lax.all_to_all(attended, "tensor", 0, 0, tiled=True).reshape(rows, width)

    payload = make_payload(head_rows, hit, id_lanes)
    own, *others = project(after(head_rows, payload), wo)
    arrived = [
        move(part, owners, lambda pair, line, s=s: (pair, (line + s) % SIDE))
        for s, part in enumerate(others, start=1)
    ]
    owned = lax.all_to_all(payload, "dp", 0, 0, tiled=True)
    down = adapter_down_weight.reshape(owner_partial * rank, width)
    up = adapter_up_weight.reshape(owner_partial * rank, width)
    partial_shrink, ids = shrink_down(after(owned, own), down, up, shares, rank)
    partials = lax.all_to_all(partial_shrink, "tensor", 0, 0, tiled=True)
    delta = expand_up(after(partials, arrived[0], arrived[2]), ids, up)
    returned = lax.all_to_all(
        delta.reshape(owners, capacity * steps, width), "dp", 0, 0, tiled=True
    ).reshape(rows, width)

    along_line = [
        own[u] + sum(part[u].astype(jnp.float32) for part in arrived) for u in range(SIDE)
    ]
    across = [
        move(
            along_line[u].astype(jnp.bfloat16),
            owners,
            lambda pair, line, u=u: ((pair + u) % SIDE, line),
        )
        for u in range(1, SIDE)
    ]
    return finish(
        hit, returned, along_line[0], across, (group_size, steps, width)
    )


def solution(mesh):
    in_specs = (
        P(("dp", "tensor"), None, None, None),
        P(("dp", "tensor"), None, None, None),
        P(("dp", "tensor"), None, None, None),
        P(("dp", "tensor")),
        P("dp"),
        P("tensor", None),
        P("dp", None, "tensor"),
        P("dp", None, "tensor"),
    )
    out_specs = P("dp", None, "tensor")
    return jax.shard_map(
        on_device, mesh=mesh, in_specs=in_specs, out_specs=out_specs, check_vma=False
    )
```

```python
import math

import jax
import jax.numpy as jnp
from jax import lax
from jax.experimental import pallas as pl
from jax.experimental.pallas import tpu as pltpu
from jax.sharding import PartitionSpec as P

NEG_FILL = -1e30
FAR_FLOPS = 20_000_000_000
SIDE = 4


def torus_place():
    tensor = lax.axis_index("tensor")
    y, x = tensor // SIDE, lax.rem(tensor, SIDE)
    odd = lax.rem(lax.axis_index("dp"), 2)
    pair, line = y + odd * (x - y), x + odd * (y - x)
    pair_stride = SIDE + odd * (1 - SIDE)
    return pair, line, pair_stride, SIDE + 1 - pair_stride


def attend_kernel(
    fill_ref, queries_ref, keys_ref, values_ref, out_ref,
    query_buf, key_buf, value_buf, score_buf, weight_buf, grouped_buf,
    query_sem, key_sem, value_sem,
):
    requests, steps, heads, head_dim = query_buf.shape
    kv_heads, cache_len = key_buf.shape[1], key_buf.shape[2]
    per_group = heads // kv_heads
    group_rows = steps * per_group
    query_copy = pltpu.make_async_copy(queries_ref, query_buf, query_sem)
    key_copies = [
        pltpu.make_async_copy(keys_ref.at[r], key_buf.at[r], key_sem.at[r]) for r in range(requests)
    ]
    value_copies = [
        pltpu.make_async_copy(values_ref.at[r], value_buf.at[r], value_sem.at[r])
        for r in range(requests)
    ]
    query_copy.start()
    for copy in key_copies:
        copy.start()
    position = lax.broadcasted_iota(jnp.int32, (group_rows, cache_len), 1)
    step_of = lax.broadcasted_iota(jnp.int32, (group_rows, cache_len), 0) // per_group
    reach = position + steps - step_of
    query_copy.wait()
    for r in range(requests):
        every = query_buf[r].astype(jnp.float32)
        key_copies[r].wait()
        value_copies[r].start()
        for k in range(kv_heads):
            grouped = every[:, k * per_group : (k + 1) * per_group, :]
            grouped = grouped.reshape(group_rows, head_dim).astype(jnp.bfloat16)
            score_buf[r * kv_heads + k] = lax.dot_general(
                grouped,
                key_buf[r, k],
                (((1,), (1,)), ((), ())),
                preferred_element_type=jnp.float32,
            )
    for r in range(requests):
        valid = reach <= fill_ref[r]
        for k in range(kv_heads):
            scores = score_buf[r * kv_heads + k] * (1.0 / math.sqrt(head_dim))
            scores = jnp.where(valid, scores, NEG_FILL)
            raised = jnp.exp(scores - jnp.max(scores, axis=1, keepdims=True))
            weights = raised * (1.0 / jnp.sum(raised, axis=1, keepdims=True))
            weight_buf[r * kv_heads + k] = weights.astype(jnp.bfloat16)
    for r in range(requests):
        value_copies[r].wait()
        for k in range(kv_heads):
            grouped_buf[k, r * group_rows : (r + 1) * group_rows] = jnp.dot(
                weight_buf[r * kv_heads + k], value_buf[r, k], preferred_element_type=jnp.float32
            ).astype(jnp.bfloat16)
    every_rows = requests * group_rows
    rows = requests * steps
    old = lax.broadcasted_iota(jnp.int32, (every_rows, every_rows), 1)
    new = lax.broadcasted_iota(jnp.int32, (every_rows, every_rows), 0)
    turn = (old == new % rows * per_group + new // rows).astype(jnp.bfloat16)
    for k in range(kv_heads):
        turned = jnp.dot(turn, grouped_buf[k], preferred_element_type=jnp.float32)
        turned = turned.astype(jnp.bfloat16)
        for g in range(per_group):
            block, at = k * (per_group // 2) + g // 2, g % 2 * head_dim
            piece = turned[g * rows : (g + 1) * rows]
            out_ref[block, :, at : at + head_dim] = piece


def attend(queries, cached_key_rows, cached_value_rows, cache_fill_length):
    requests, steps, heads, head_dim = queries.shape
    kv_heads, cache_len = cached_key_rows.shape[1:3]
    blocks, rows = heads // 2, requests * steps
    pairs, group_rows = requests * kv_heads, steps * heads // kv_heads
    distant = pl.BlockSpec(memory_space=pl.ANY)
    return pl.pallas_call(
        attend_kernel,
        in_specs=[pl.BlockSpec(memory_space=pltpu.SMEM)] + [distant] * 3,
        out_specs=pl.BlockSpec(memory_space=pltpu.VMEM),
        out_shape=jax.ShapeDtypeStruct((blocks, rows, 2 * head_dim), jnp.bfloat16),
        scratch_shapes=[
            pltpu.VMEM(queries.shape, jnp.bfloat16),
            pltpu.VMEM(cached_key_rows.shape, jnp.bfloat16),
            pltpu.VMEM(cached_value_rows.shape, jnp.bfloat16),
            pltpu.VMEM((pairs, group_rows, cache_len), jnp.float32),
            pltpu.VMEM((pairs, group_rows, cache_len), jnp.bfloat16),
            pltpu.VMEM((kv_heads, requests * group_rows, head_dim), jnp.bfloat16),
            pltpu.SemaphoreType.DMA,
            pltpu.SemaphoreType.DMA((requests,)),
            pltpu.SemaphoreType.DMA((requests,)),
        ],
        compiler_params=pltpu.CompilerParams(vmem_limit_bytes=60 * 1024 * 1024),
        cost_estimate=pl.CostEstimate(
            flops=4 * rows * heads * cache_len * head_dim,
            bytes_accessed=2 * 2 * cached_key_rows.size,
            transcendentals=rows * heads * cache_len,
        ),
        name="attend",
    )(cache_fill_length, queries, cached_key_rows, cached_value_rows)


def slot_kernel(slots_ref, locals_ref, hit_ref, ids_ref):
    owners, capacity, lanes = ids_ref.shape
    rows = hit_ref.shape[0]
    slot = lax.broadcasted_iota(jnp.int32, (rows, rows), 0)
    hit_ref[...] = (slot == slots_ref[...]).astype(jnp.bfloat16)
    steps = rows // owners // capacity
    wanted = lax.broadcasted_iota(jnp.int32, (owners * capacity, 1), 0) * steps
    pick = (wanted == slots_ref[...]).astype(jnp.bfloat16)
    ids = locals_ref[...].astype(jnp.float32).astype(jnp.bfloat16)
    spread = lax.dot_general(
        pick,
        jnp.broadcast_to(ids, (lanes, rows)),
        (((1,), (1,)), ((), ())),
        preferred_element_type=jnp.float32,
    )
    ids_ref[...] = spread.reshape(owners, capacity, lanes).astype(jnp.bfloat16)


def slot_map(row_slots, row_locals, owners, capacity):
    rows = row_slots.shape[1]
    resident = pl.BlockSpec(memory_space=pltpu.VMEM)
    return pl.pallas_call(
        slot_kernel,
        in_specs=[resident] * 2,
        out_specs=[resident] * 2,
        out_shape=[
            jax.ShapeDtypeStruct((rows, rows), jnp.bfloat16),
            jax.ShapeDtypeStruct((owners, capacity, 128), jnp.bfloat16),
        ],
        compiler_params=pltpu.CompilerParams(vmem_limit_bytes=16 * 1024 * 1024),
        cost_estimate=pl.CostEstimate(
            flops=2 * rows * rows * 128, bytes_accessed=4 * rows * rows, transcendentals=0
        ),
        name="slot_map",
    )(row_slots, row_locals)


def payload_kernel(rows_ref, hit_ref, ids_ref, out_ref):
    owners, tiles, tile_rows, lanes = out_ref.shape
    run = (tiles - 1) // 2
    part = jnp.dot(hit_ref[...], rows_ref[...], preferred_element_type=jnp.float32)
    for half in range(2):
        piece = part[:, half * lanes : (half + 1) * lanes].reshape(owners, run, tile_rows, lanes)
        out_ref[:, half * run : (half + 1) * run] = piece.astype(jnp.bfloat16)
    out_ref[:, tiles - 1] = ids_ref[...]


def make_payload(head_rows, hit, ids):
    rows, width = head_rows.shape
    owners, tile_rows, lanes = ids.shape
    tiles = rows // owners // tile_rows * (width // lanes) + 1
    resident = pl.BlockSpec(memory_space=pltpu.VMEM)
    return pl.pallas_call(
        payload_kernel,
        in_specs=[resident] * 3,
        out_specs=resident,
        out_shape=jax.ShapeDtypeStruct((owners, tiles, tile_rows, lanes), jnp.bfloat16),
        compiler_params=pltpu.CompilerParams(vmem_limit_bytes=16 * 1024 * 1024),
        cost_estimate=pl.CostEstimate(
            flops=2 * rows * rows * width, bytes_accessed=8 * rows * width, transcendentals=0
        ),
        name="make_payload",
    )(head_rows, hit, ids)


def project_kernel(rows_ref, wo_ref, own_ref, far_ref, near_1_ref, near_3_ref, *scratch):
    own_buf, far_buf, sems = scratch
    pair, line, pair_stride, line_stride = torus_place()
    width = rows_ref.shape[1]
    copies = []
    for s, part_ref in ((0, own_buf), (2, far_buf), (1, near_1_ref), (3, near_3_ref)):
        along = lax.rem(line + s, SIDE)
        for u in range(SIDE):
            across = lax.rem(pair + u, SIDE)
            at = pl.multiple_of((across * pair_stride + along * line_stride) * width, width)
            part = jnp.dot(
                rows_ref[...], wo_ref[:, pl.ds(at, width)], preferred_element_type=jnp.float32
            )
            part_ref[u] = part.astype(part_ref.dtype)
        if s % 2 == 0:
            target = own_ref if s == 0 else far_ref
            copies.append(pltpu.make_async_copy(part_ref, target, sems.at[s // 2]))
            copies[-1].start()
    for copy in copies:
        copy.wait()


def project(head_rows, wo):
    rows, depth = head_rows.shape
    width = wo.shape[1] // (SIDE * SIDE)
    shape = (SIDE, rows, width)
    resident = pl.BlockSpec(memory_space=pltpu.VMEM)
    distant = pl.BlockSpec(memory_space=pltpu.HBM)
    own, far, near_1, near_3 = pl.pallas_call(
        project_kernel,
        in_specs=[resident] * 2,
        out_specs=[distant] * 2 + [resident] * 2,
        out_shape=[pltpu.HBM(shape, jnp.bfloat16)] * 2
        + [jax.ShapeDtypeStruct(shape, jnp.bfloat16)] * 2,
        scratch_shapes=[
            pltpu.VMEM(shape, jnp.bfloat16),
            pltpu.VMEM(shape, jnp.bfloat16),
            pltpu.SemaphoreType.DMA((2,)),
        ],
        compiler_params=pltpu.CompilerParams(vmem_limit_bytes=16 * 1024 * 1024),
        cost_estimate=pl.CostEstimate(
            flops=2 * rows * depth * wo.shape[1],
            bytes_accessed=2 * wo.size + 3 * rows * wo.shape[1],
            transcendentals=0,
        ),
        name="project",
    )(head_rows, wo)
    return own, near_1, far, near_3


def down_kernel(owned_ref, down_ref, up_ref, out_ref, ids_ref):
    del up_ref
    sources, tiles, capacity, lanes = owned_ref.shape
    run = (tiles - 1) // 2
    rank, rows = out_ref.shape[1:]
    adapters = down_ref.shape[0] // rank
    every = 0.0
    for half in range(2):
        piece = owned_ref[:, half * run : (half + 1) * run].astype(jnp.float32)
        every += lax.dot_general(
            down_ref[:, half * lanes : (half + 1) * lanes],
            piece.reshape(rows, lanes).astype(jnp.bfloat16),
            (((1,), (1,)), ((), ())),
            preferred_element_type=jnp.float32,
        )
    tile = owned_ref[:, tiles - 1].astype(jnp.float32)
    ids = jnp.concatenate(
        [
            jnp.broadcast_to(tile[:, k : k + 1], (sources, rows // sources // capacity, lanes))
            for k in range(capacity)
        ],
        axis=1,
    ).reshape(rows, lanes)
    ids_ref[...] = ids
    adapter = lax.broadcasted_iota(jnp.int32, (adapters, rank, rows), 0).astype(jnp.float32)
    chosen = adapter == jnp.transpose(ids)[:1].reshape(1, 1, rows)
    part = jnp.sum(jnp.where(chosen, every.reshape(adapters, rank, rows), 0.0), axis=0)
    for share in range(out_ref.shape[0]):
        out_ref[share] = part.astype(out_ref.dtype)


def shrink_down(owned, down, up, shares, rank):
    sources, tiles, tile_rows, lanes = owned.shape
    rows = sources * (tiles - 1) // 2 * tile_rows
    resident = pl.BlockSpec(memory_space=pltpu.VMEM)
    return pl.pallas_call(
        down_kernel,
        in_specs=[resident] * 3,
        out_specs=[resident] * 2,
        out_shape=[
            jax.ShapeDtypeStruct((shares, rank, rows), jnp.bfloat16),
            jax.ShapeDtypeStruct((rows, lanes), jnp.float32),
        ],
        compiler_params=pltpu.CompilerParams(vmem_limit_bytes=16 * 1024 * 1024),
        cost_estimate=pl.CostEstimate(
            flops=2 * rows * down.size, bytes_accessed=4 * down.size, transcendentals=0
        ),
        name="shrink_down",
    )(owned, down, up)


def up_kernel(partials_ref, ids_ref, up_ref, out_ref):
    shares, rank, rows = partials_ref.shape
    maps = up_ref.shape[0]
    lanes = ids_ref.shape[1]
    shrink = partials_ref[0].astype(jnp.float32)
    for share in range(1, shares):
        shrink += partials_ref[share].astype(jnp.float32)
    fold = lax.broadcasted_iota(jnp.int32, (rank, maps), 1) % rank
    fold = (fold == lax.broadcasted_iota(jnp.int32, (rank, maps), 0)).astype(jnp.bfloat16)
    spread = lax.dot_general(
        shrink.astype(jnp.bfloat16),
        fold,
        (((0,), (0,)), ((), ())),
        preferred_element_type=jnp.float32,
    )
    ids = jnp.concatenate([ids_ref[...]] * (maps // lanes), axis=1)
    adapter = (lax.broadcasted_iota(jnp.int32, (1, maps), 1) // rank).astype(jnp.float32)
    out_ref[...] = jnp.dot(
        jnp.where(adapter == ids, spread, 0.0).astype(jnp.bfloat16),
        up_ref[...],
        preferred_element_type=jnp.float32,
    ).astype(jnp.bfloat16)


def expand_up(partials, ids, up):
    rows = partials.shape[2]
    resident = pl.BlockSpec(memory_space=pltpu.VMEM)
    return pl.pallas_call(
        up_kernel,
        in_specs=[resident] * 3,
        out_specs=resident,
        out_shape=jax.ShapeDtypeStruct((rows, up.shape[1]), jnp.bfloat16),
        compiler_params=pltpu.CompilerParams(vmem_limit_bytes=16 * 1024 * 1024),
        cost_estimate=pl.CostEstimate(
            flops=FAR_FLOPS, bytes_accessed=4 * up.size, transcendentals=0
        ),
        name="expand_up",
    )(partials, ids, up)


def finish_kernel(hit_ref, returned_ref, base_ref, *refs):
    across_refs, out_ref = refs[:-1], refs[-1]
    delta = lax.dot_general(
        hit_ref[...], returned_ref[...], (((0,), (0,)), ((), ())), preferred_element_type=jnp.float32
    )
    total = base_ref[...] + delta
    for across_ref in across_refs:
        total += across_ref[...].astype(jnp.float32)
    out_ref[...] = total.reshape(out_ref.shape).astype(out_ref.dtype)


def finish(hit, returned, base, across, out_shape):
    resident = pl.BlockSpec(memory_space=pltpu.VMEM)
    return pl.pallas_call(
        finish_kernel,
        in_specs=[resident] * (3 + len(across)),
        out_specs=resident,
        out_shape=jax.ShapeDtypeStruct(out_shape, jnp.bfloat16),
        compiler_params=pltpu.CompilerParams(vmem_limit_bytes=16 * 1024 * 1024),
        cost_estimate=pl.CostEstimate(
            flops=2 * returned.size * returned.shape[0],
            bytes_accessed=8 * returned.size,
            transcendentals=0,
        ),
        name="finish",
    )(hit, returned, base, *across)


def move(value, owners, target):
    pairs = []
    for d in range(owners):
        for pair in range(SIDE):
            for line in range(SIDE):
                to_pair, to_line = target(pair, line)
                if d % 2 == 0:
                    here, there = pair * SIDE + line, to_pair * SIDE + to_line
                else:
                    here, there = line * SIDE + pair, to_line * SIDE + to_pair
                pairs.append((d * SIDE * SIDE + here, d * SIDE * SIDE + there))
    return lax.ppermute(value, ("dp", "tensor"), pairs)


def after(value, *earlier):
    return lax.optimization_barrier((value,) + earlier)[0]


def on_device(
    queries,
    cached_key_rows,
    cached_value_rows,
    cache_fill_length,
    request_adapters,
    wo,
    adapter_down_weight,
    adapter_up_weight,
):
    owners = lax.axis_size("dp")
    shares = lax.axis_size("tensor")
    group_size = request_adapters.shape[0]
    owner_partial, rank, width = adapter_down_weight.shape
    capacity = group_size // owners
    steps = queries.shape[1]
    rows = group_size * steps

    owner_ids = request_adapters // owner_partial
    local_ids = request_adapters % owner_partial
    order = jnp.arange(group_size, dtype=jnp.int32)
    earlier = (owner_ids[:, None] == owner_ids[None, :]) & (order[:, None] > order[None, :])
    slots = owner_ids * capacity + jnp.sum(earlier.astype(jnp.int32), axis=1)
    row_slots = (slots[:, None] * steps + jnp.arange(steps, dtype=jnp.int32)).reshape(1, rows)
    row_locals = jnp.repeat(local_ids, steps)[None, :]
    hit, id_lanes = slot_map(row_slots, row_locals, owners, capacity)

    attended = attend(queries, cached_key_rows, cached_value_rows, cache_fill_length)
    head_rows = lax.all_to_all(attended, "tensor", 0, 0, tiled=True).reshape(rows, width)

    payload = make_payload(head_rows, hit, id_lanes)
    own, *others = project(after(head_rows, payload), wo)
    arrived = [
        move(part, owners, lambda pair, line, s=s: (pair, (line + s) % SIDE))
        for s, part in enumerate(others, start=1)
    ]
    owned = lax.all_to_all(payload, "dp", 0, 0, tiled=True)
    down = adapter_down_weight.reshape(owner_partial * rank, width)
    up = adapter_up_weight.reshape(owner_partial * rank, width)
    partial_shrink, ids = shrink_down(after(owned, own), down, up, shares, rank)
    partials = lax.all_to_all(partial_shrink, "tensor", 0, 0, tiled=True)
    delta = expand_up(after(partials, arrived[0], arrived[2]), ids, up)
    returned = lax.all_to_all(
        delta.reshape(owners, capacity * steps, width), "dp", 0, 0, tiled=True
    ).reshape(rows, width)

    along_line = [
        own[u].astype(jnp.float32) + sum(part[u].astype(jnp.float32) for part in arrived) for u in range(SIDE)
    ]
    across = [
        move(
            along_line[u].astype(jnp.bfloat16),
            owners,
            lambda pair, line, u=u: ((pair + u) % SIDE, line),
        )
        for u in range(1, SIDE)
    ]
    return finish(
        hit, returned, along_line[0], across, (group_size, steps, width)
    )


def solution(mesh):
    in_specs = (
        P(("dp", "tensor"), None, None, None),
        P(("dp", "tensor"), None, None, None),
        P(("dp", "tensor"), None, None, None),
        P(("dp", "tensor")),
        P("dp"),
        P("tensor", None),
        P("dp", None, "tensor"),
        P("dp", None, "tensor"),
    )
    out_specs = P("dp", None, "tensor")
    return jax.shard_map(
        on_device, mesh=mesh, in_specs=in_specs, out_specs=out_specs, check_vma=False
    )
```

```python
import math

import jax
import jax.numpy as jnp
from jax import lax
from jax.experimental import pallas as pl
from jax.experimental.pallas import tpu as pltpu
from jax.sharding import PartitionSpec as P

NEG_FILL = -1e30
FAR_FLOPS = 20_000_000_000
SIDE = 4


def torus_place():
    tensor = lax.axis_index("tensor")
    y, x = tensor // SIDE, lax.rem(tensor, SIDE)
    odd = lax.rem(lax.axis_index("dp"), 2)
    pair, line = y + odd * (x - y), x + odd * (y - x)
    pair_stride = SIDE + odd * (1 - SIDE)
    return pair, line, pair_stride, SIDE + 1 - pair_stride


def attend_kernel(
    fill_ref, queries_ref, keys_ref, values_ref, out_ref,
    query_buf, key_buf, value_buf, score_buf, weight_buf, grouped_buf,
    query_sem, key_sem, value_sem,
):
    requests, steps, heads, head_dim = query_buf.shape
    kv_heads, cache_len = key_buf.shape[1], key_buf.shape[2]
    per_group = heads // kv_heads
    group_rows = steps * per_group
    query_copy = pltpu.make_async_copy(queries_ref, query_buf, query_sem)
    key_copies = [
        pltpu.make_async_copy(keys_ref.at[r], key_buf.at[r], key_sem.at[r]) for r in range(requests)
    ]
    value_copies = [
        pltpu.make_async_copy(values_ref.at[r], value_buf.at[r], value_sem.at[r])
        for r in range(requests)
    ]
    query_copy.start()
    for copy in key_copies:
        copy.start()
    position = lax.broadcasted_iota(jnp.int32, (group_rows, cache_len), 1)
    step_of = lax.broadcasted_iota(jnp.int32, (group_rows, cache_len), 0) // per_group
    reach = position + steps - step_of
    query_copy.wait()
    for r in range(requests):
        every = query_buf[r].astype(jnp.float32)
        key_copies[r].wait()
        value_copies[r].start()
        for k in range(kv_heads):
            grouped = every[:, k * per_group : (k + 1) * per_group, :]
            grouped = grouped.reshape(group_rows, head_dim).astype(jnp.bfloat16)
            score_buf[r * kv_heads + k] = lax.dot_general(
                grouped,
                key_buf[r, k],
                (((1,), (1,)), ((), ())),
                preferred_element_type=jnp.float32,
            )
    for r in range(requests):
        valid = reach <= fill_ref[r]
        for k in range(kv_heads):
            scores = score_buf[r * kv_heads + k] * (1.0 / math.sqrt(head_dim))
            scores = jnp.where(valid, scores, NEG_FILL)
            raised = jnp.exp(scores - jnp.max(scores, axis=1, keepdims=True))
            weights = raised * (1.0 / jnp.sum(raised, axis=1, keepdims=True))
            weight_buf[r * kv_heads + k] = weights.astype(jnp.bfloat16)
    for r in range(requests):
        value_copies[r].wait()
        for k in range(kv_heads):
            grouped_buf[k, r * group_rows : (r + 1) * group_rows] = jnp.dot(
                weight_buf[r * kv_heads + k], value_buf[r, k], preferred_element_type=jnp.float32
            ).astype(jnp.bfloat16)
    every_rows = requests * group_rows
    rows = requests * steps
    old = lax.broadcasted_iota(jnp.int32, (every_rows, every_rows), 1)
    new = lax.broadcasted_iota(jnp.int32, (every_rows, every_rows), 0)
    turn = (old == new % rows * per_group + new // rows).astype(jnp.bfloat16)
    for k in range(kv_heads):
        turned = jnp.dot(turn, grouped_buf[k], preferred_element_type=jnp.float32)
        turned = turned.astype(jnp.bfloat16)
        for g in range(per_group):
            block, at = k * (per_group // 2) + g // 2, g % 2 * head_dim
            piece = turned[g * rows : (g + 1) * rows]
            out_ref[block, :, at : at + head_dim] = piece


def attend(queries, cached_key_rows, cached_value_rows, cache_fill_length):
    requests, steps, heads, head_dim = queries.shape
    kv_heads, cache_len = cached_key_rows.shape[1:3]
    blocks, rows = heads // 2, requests * steps
    pairs, group_rows = requests * kv_heads, steps * heads // kv_heads
    distant = pl.BlockSpec(memory_space=pl.ANY)
    return pl.pallas_call(
        attend_kernel,
        in_specs=[pl.BlockSpec(memory_space=pltpu.SMEM)] + [distant] * 3,
        out_specs=pl.BlockSpec(memory_space=pltpu.VMEM),
        out_shape=jax.ShapeDtypeStruct((blocks, rows, 2 * head_dim), jnp.bfloat16),
        scratch_shapes=[
            pltpu.VMEM(queries.shape, jnp.bfloat16),
            pltpu.VMEM(cached_key_rows.shape, jnp.bfloat16),
            pltpu.VMEM(cached_value_rows.shape, jnp.bfloat16),
            pltpu.VMEM((pairs, group_rows, cache_len), jnp.float32),
            pltpu.VMEM((pairs, group_rows, cache_len), jnp.bfloat16),
            pltpu.VMEM((kv_heads, requests * group_rows, head_dim), jnp.bfloat16),
            pltpu.SemaphoreType.DMA,
            pltpu.SemaphoreType.DMA((requests,)),
            pltpu.SemaphoreType.DMA((requests,)),
        ],
        compiler_params=pltpu.CompilerParams(vmem_limit_bytes=60 * 1024 * 1024),
        cost_estimate=pl.CostEstimate(
            flops=4 * rows * heads * cache_len * head_dim,
            bytes_accessed=2 * 2 * cached_key_rows.size,
            transcendentals=rows * heads * cache_len,
        ),
        name="attend",
    )(cache_fill_length, queries, cached_key_rows, cached_value_rows)


def slot_kernel(slots_ref, locals_ref, hit_ref, ids_ref):
    owners, capacity, lanes = ids_ref.shape
    rows = hit_ref.shape[0]
    slot = lax.broadcasted_iota(jnp.int32, (rows, rows), 0)
    hit_ref[...] = (slot == slots_ref[...]).astype(jnp.bfloat16)
    steps = rows // owners // capacity
    wanted = lax.broadcasted_iota(jnp.int32, (owners * capacity, 1), 0) * steps
    pick = (wanted == slots_ref[...]).astype(jnp.bfloat16)
    ids = locals_ref[...].astype(jnp.float32).astype(jnp.bfloat16)
    spread = lax.dot_general(
        pick,
        jnp.broadcast_to(ids, (lanes, rows)),
        (((1,), (1,)), ((), ())),
        preferred_element_type=jnp.float32,
    )
    ids_ref[...] = spread.reshape(owners, capacity, lanes).astype(jnp.bfloat16)


def slot_map(row_slots, row_locals, owners, capacity):
    rows = row_slots.shape[1]
    resident = pl.BlockSpec(memory_space=pltpu.VMEM)
    return pl.pallas_call(
        slot_kernel,
        in_specs=[resident] * 2,
        out_specs=[resident] * 2,
        out_shape=[
            jax.ShapeDtypeStruct((rows, rows), jnp.bfloat16),
            jax.ShapeDtypeStruct((owners, capacity, 128), jnp.bfloat16),
        ],
        compiler_params=pltpu.CompilerParams(vmem_limit_bytes=16 * 1024 * 1024),
        cost_estimate=pl.CostEstimate(
            flops=2 * rows * rows * 128, bytes_accessed=4 * rows * rows, transcendentals=0
        ),
        name="slot_map",
    )(row_slots, row_locals)


def payload_kernel(rows_ref, hit_ref, ids_ref, out_ref):
    owners, tiles, tile_rows, lanes = out_ref.shape
    run = (tiles - 1) // 2
    part = jnp.dot(hit_ref[...], rows_ref[...], preferred_element_type=jnp.float32)
    for half in range(2):
        piece = part[:, half * lanes : (half + 1) * lanes].reshape(owners, run, tile_rows, lanes)
        out_ref[:, half * run : (half + 1) * run] = piece.astype(jnp.bfloat16)
    out_ref[:, tiles - 1] = ids_ref[...]


def make_payload(head_rows, hit, ids):
    rows, width = head_rows.shape
    owners, tile_rows, lanes = ids.shape
    tiles = rows // owners // tile_rows * (width // lanes) + 1
    resident = pl.BlockSpec(memory_space=pltpu.VMEM)
    return pl.pallas_call(
        payload_kernel,
        in_specs=[resident] * 3,
        out_specs=resident,
        out_shape=jax.ShapeDtypeStruct((owners, tiles, tile_rows, lanes), jnp.bfloat16),
        compiler_params=pltpu.CompilerParams(vmem_limit_bytes=16 * 1024 * 1024),
        cost_estimate=pl.CostEstimate(
            flops=2 * rows * rows * width, bytes_accessed=8 * rows * width, transcendentals=0
        ),
        name="make_payload",
    )(head_rows, hit, ids)


def project_kernel(rows_ref, wo_ref, own_ref, far_ref, near_1_ref, near_3_ref, *scratch):
    own_buf, far_buf, sems = scratch
    pair, line, pair_stride, line_stride = torus_place()
    width = rows_ref.shape[1]
    copies = []
    for s, part_ref in ((0, own_buf), (2, far_buf), (1, near_1_ref), (3, near_3_ref)):
        along = lax.rem(line + s, SIDE)
        for u in range(SIDE):
            across = lax.rem(pair + u, SIDE)
            at = pl.multiple_of((across * pair_stride + along * line_stride) * width, width)
            part = jnp.dot(
                rows_ref[...], wo_ref[:, pl.ds(at, width)], preferred_element_type=jnp.float32
            )
            part_ref[u] = part.astype(part_ref.dtype)
        if s % 2 == 0:
            target = own_ref if s == 0 else far_ref
            copies.append(pltpu.make_async_copy(part_ref, target, sems.at[s // 2]))
            copies[-1].start()
    for copy in copies:
        copy.wait()


def project(head_rows, wo):
    rows, depth = head_rows.shape
    width = wo.shape[1] // (SIDE * SIDE)
    shape = (SIDE, rows, width)
    resident = pl.BlockSpec(memory_space=pltpu.VMEM)
    distant = pl.BlockSpec(memory_space=pltpu.HBM)
    own, far, near_1, near_3 = pl.pallas_call(
        project_kernel,
        in_specs=[resident] * 2,
        out_specs=[distant] * 2 + [resident] * 2,
        out_shape=[pltpu.HBM(shape, jnp.float32), pltpu.HBM(shape, jnp.bfloat16)]
        + [jax.ShapeDtypeStruct(shape, jnp.bfloat16)] * 2,
        scratch_shapes=[
            pltpu.VMEM(shape, jnp.float32),
            pltpu.VMEM(shape, jnp.bfloat16),
            pltpu.SemaphoreType.DMA((2,)),
        ],
        compiler_params=pltpu.CompilerParams(vmem_limit_bytes=16 * 1024 * 1024),
        cost_estimate=pl.CostEstimate(
            flops=2 * rows * depth * wo.shape[1],
            bytes_accessed=2 * wo.size + 3 * rows * wo.shape[1],
            transcendentals=0,
        ),
        name="project",
    )(head_rows, wo)
    return own, near_1, far, near_3


def down_kernel(owned_ref, down_ref, up_ref, out_ref, ids_ref):
    del up_ref
    sources, tiles, capacity, lanes = owned_ref.shape
    run = (tiles - 1) // 2
    rank, rows = out_ref.shape[1:]
    adapters = down_ref.shape[0] // rank
    every = 0.0
    for half in range(2):
        piece = owned_ref[:, half * run : (half + 1) * run].astype(jnp.float32)
        every += lax.dot_general(
            down_ref[:, half * lanes : (half + 1) * lanes],
            piece.reshape(rows, lanes).astype(jnp.bfloat16),
            (((1,), (1,)), ((), ())),
            preferred_element_type=jnp.float32,
        )
    tile = owned_ref[:, tiles - 1].astype(jnp.float32)
    ids = jnp.concatenate(
        [
            jnp.broadcast_to(tile[:, k : k + 1], (sources, rows // sources // capacity, lanes))
            for k in range(capacity)
        ],
        axis=1,
    ).reshape(rows, lanes)
    ids_ref[...] = ids
    adapter = lax.broadcasted_iota(jnp.int32, (adapters, rank, rows), 0).astype(jnp.float32)
    chosen = adapter == jnp.transpose(ids)[:1].reshape(1, 1, rows)
    part = jnp.sum(jnp.where(chosen, every.reshape(adapters, rank, rows), 0.0), axis=0)
    for share in range(out_ref.shape[0]):
        out_ref[share] = part.astype(out_ref.dtype)


def shrink_down(owned, down, up, shares, rank):
    sources, tiles, tile_rows, lanes = owned.shape
    rows = sources * (tiles - 1) // 2 * tile_rows
    resident = pl.BlockSpec(memory_space=pltpu.VMEM)
    return pl.pallas_call(
        down_kernel,
        in_specs=[resident] * 3,
        out_specs=[resident] * 2,
        out_shape=[
            jax.ShapeDtypeStruct((shares, rank, rows), jnp.bfloat16),
            jax.ShapeDtypeStruct((rows, lanes), jnp.float32),
        ],
        compiler_params=pltpu.CompilerParams(vmem_limit_bytes=16 * 1024 * 1024),
        cost_estimate=pl.CostEstimate(
            flops=2 * rows * down.size, bytes_accessed=4 * down.size, transcendentals=0
        ),
        name="shrink_down",
    )(owned, down, up)


def up_kernel(partials_ref, ids_ref, up_ref, out_ref):
    shares, rank, rows = partials_ref.shape
    maps = up_ref.shape[0]
    lanes = ids_ref.shape[1]
    shrink = partials_ref[0].astype(jnp.float32)
    for share in range(1, shares):
        shrink += partials_ref[share].astype(jnp.float32)
    fold = lax.broadcasted_iota(jnp.int32, (rank, maps), 1) % rank
    fold = (fold == lax.broadcasted_iota(jnp.int32, (rank, maps), 0)).astype(jnp.bfloat16)
    spread = lax.dot_general(
        shrink.astype(jnp.bfloat16),
        fold,
        (((0,), (0,)), ((), ())),
        preferred_element_type=jnp.float32,
    )
    ids = jnp.concatenate([ids_ref[...]] * (maps // lanes), axis=1)
    adapter = (lax.broadcasted_iota(jnp.int32, (1, maps), 1) // rank).astype(jnp.float32)
    out_ref[...] = jnp.dot(
        jnp.where(adapter == ids, spread, 0.0).astype(jnp.bfloat16),
        up_ref[...],
        preferred_element_type=jnp.float32,
    ).astype(jnp.bfloat16)


def expand_up(partials, ids, up):
    rows = partials.shape[2]
    resident = pl.BlockSpec(memory_space=pltpu.VMEM)
    return pl.pallas_call(
        up_kernel,
        in_specs=[resident] * 3,
        out_specs=resident,
        out_shape=jax.ShapeDtypeStruct((rows, up.shape[1]), jnp.bfloat16),
        compiler_params=pltpu.CompilerParams(vmem_limit_bytes=16 * 1024 * 1024),
        cost_estimate=pl.CostEstimate(
            flops=FAR_FLOPS, bytes_accessed=4 * up.size, transcendentals=0
        ),
        name="expand_up",
    )(partials, ids, up)


def finish_kernel(hit_ref, returned_ref, base_ref, *refs):
    across_refs, out_ref = refs[:-1], refs[-1]
    delta = lax.dot_general(
        hit_ref[...], returned_ref[...], (((0,), (0,)), ((), ())), preferred_element_type=jnp.float32
    )
    total = base_ref[...] + delta
    for across_ref in across_refs:
        total += across_ref[...].astype(jnp.float32)
    out_ref[...] = total.reshape(out_ref.shape).astype(out_ref.dtype)


def finish(hit, returned, base, across, out_shape):
    resident = pl.BlockSpec(memory_space=pltpu.VMEM)
    return pl.pallas_call(
        finish_kernel,
        in_specs=[resident] * (3 + len(across)),
        out_specs=resident,
        out_shape=jax.ShapeDtypeStruct(out_shape, jnp.bfloat16),
        compiler_params=pltpu.CompilerParams(vmem_limit_bytes=16 * 1024 * 1024),
        cost_estimate=pl.CostEstimate(
            flops=2 * returned.size * returned.shape[0],
            bytes_accessed=8 * returned.size,
            transcendentals=0,
        ),
        name="finish",
    )(hit, returned, base, *across)


def move(value, owners, target):
    pairs = []
    for d in range(owners):
        for pair in range(SIDE):
            for line in range(SIDE):
                to_pair, to_line = target(pair, line)
                if d % 2 == 0:
                    here, there = pair * SIDE + line, to_pair * SIDE + to_line
                else:
                    here, there = line * SIDE + pair, to_line * SIDE + to_pair
                pairs.append((d * SIDE * SIDE + here, d * SIDE * SIDE + there))
    return lax.ppermute(value, ("dp", "tensor"), pairs)


def after(value, *earlier):
    return lax.optimization_barrier((value,) + earlier)[0]


def on_device(
    queries,
    cached_key_rows,
    cached_value_rows,
    cache_fill_length,
    request_adapters,
    wo,
    adapter_down_weight,
    adapter_up_weight,
):
    owners = lax.axis_size("dp")
    shares = lax.axis_size("tensor")
    group_size = request_adapters.shape[0]
    owner_partial, rank, width = adapter_down_weight.shape
    capacity = group_size // owners
    steps = queries.shape[1]
    rows = group_size * steps

    owner_ids = request_adapters // owner_partial
    local_ids = request_adapters % owner_partial
    order = jnp.arange(group_size, dtype=jnp.int32)
    earlier = (owner_ids[:, None] == owner_ids[None, :]) & (order[:, None] > order[None, :])
    slots = owner_ids * capacity + jnp.sum(earlier.astype(jnp.int32), axis=1)
    row_slots = (slots[:, None] * steps + jnp.arange(steps, dtype=jnp.int32)).reshape(1, rows)
    row_locals = jnp.repeat(local_ids, steps)[None, :]
    hit, id_lanes = slot_map(row_slots, row_locals, owners, capacity)

    attended = attend(queries, cached_key_rows, cached_value_rows, cache_fill_length)
    head_rows = lax.all_to_all(attended, "tensor", 0, 0, tiled=True).reshape(rows, width)

    payload = make_payload(head_rows, hit, id_lanes)
    own, *others = project(after(head_rows, payload), wo)
    arrived = [
        move(part, owners, lambda pair, line, s=s: (pair, (line + s) % SIDE))
        for s, part in enumerate(others, start=1)
    ]
    owned = lax.all_to_all(payload, "dp", 0, 0, tiled=True)
    down = adapter_down_weight.reshape(owner_partial * rank, width)
    up = adapter_up_weight.reshape(owner_partial * rank, width)
    partial_shrink, ids = shrink_down(after(owned, own), down, up, shares, rank)
    partials = lax.all_to_all(partial_shrink, "tensor", 0, 0, tiled=True)
    delta = expand_up(after(partials, arrived[0], arrived[2]), ids, up)
    returned = lax.all_to_all(
        delta.reshape(owners, capacity * steps, width), "dp", 0, 0, tiled=True
    ).reshape(rows, width)

    to_send = [
        (own[u] + sum(part[u].astype(jnp.float32) for part in arrived)).astype(jnp.bfloat16)
        for u in range(1, SIDE)
    ]
    kept_parts = lax.optimization_barrier((own[0], [part[0] for part in arrived], to_send))
    kept = kept_parts[0] + sum(part.astype(jnp.float32) for part in kept_parts[1])
    across = [
        move(
            to_send[u - 1],
            owners,
            lambda pair, line, u=u: ((pair + u) % SIDE, line),
        )
        for u in range(1, SIDE)
    ]
    return finish(
        hit, returned, kept, across, (group_size, steps, width)
    )


def solution(mesh):
    in_specs = (
        P(("dp", "tensor"), None, None, None),
        P(("dp", "tensor"), None, None, None),
        P(("dp", "tensor"), None, None, None),
        P(("dp", "tensor")),
        P("dp"),
        P("tensor", None),
        P("dp", None, "tensor"),
        P("dp", None, "tensor"),
    )
    out_specs = P("dp", None, "tensor")
    return jax.shard_map(
        on_device, mesh=mesh, in_specs=in_specs, out_specs=out_specs, check_vma=False
    )
```
